128 devices in a mesh: row: 8 (over z, core), col: 16 (over y, x).
Axes of the slice: x: 4, y: 4, z: 4, core: 2. Of those that a mesh axis runs over, the one named last changes fastest.
Arguments:
- spectra: bfloat16 [2048, 32, 128], P(('row', 'col')), may hold values from -6 to 6
- pair_bins: int32 [2048, 2048], P('row', 'col'), may hold values from 0 to 255
- row_subs: int32 [8, 32], P('row'), may hold values from 0 to 127, as said below
- station_subs: int32 [2048, 8], replicated, may hold values from 0 to 127, as said below
- kernel: bfloat16 [32, 256, 256], replicated, may hold values from -0.375 to 0.375
Outputs:
- spectrum: float32 [128, 32, 256], P(('row', 'col'))
The draws below stay inside these ranges and needn't reach their ends.
Inputs may be any that keep to these rules, and one draw needn't show every extreme that they name: `row_subs`: each row lists 32 distinct subarrays; each subarray is listed for exactly two row blocks. `station_subs`: each station names 8 distinct subarrays, all listed in row_subs for the station's row block.
All inputs are finite; a program needn't handle non-finite values.
Results may differ from the reference program's by a relative error of at most 0.0039.
Values may be sent and summed in bfloat16 or wider, within the bound.
No kernel may reach another device: no remote copies, remote signals or barrier semaphores. Data moves between devices by JAX's collectives and lax.ppermute only.
A program may use at most 64 MiB of HBM per device.

```python
import jax
import jax.numpy as jnp
from jax import lax

F = 32
WIN2 = 128
NBIN = 256
V = 256
MS = 8
STA = 2048
ROW_STA = 256
NSUB = 128
LS = 32
N_ROW = 8
N_COL = 16


def make_lists(key):
    shuffled = jax.random.permutation(jax.random.fold_in(key, 11), NSUB).astype(jnp.int32)
    half_list = LS // 2
    quarter = half_list // 4
    row_ids = jnp.arange(N_ROW, dtype=jnp.int32)[:, None]
    slot_ids = jnp.arange(LS, dtype=jnp.int32)[None, :]
    inner = slot_ids % half_list
    far_rows = jnp.where(inner < quarter, row_ids + N_ROW - 1, jnp.where(inner < 2 * quarter, row_ids + 1, row_ids + N_ROW // 2)) % N_ROW
    block_ids = jnp.where(slot_ids < half_list, row_ids, far_rows)
    places = block_ids * half_list + inner
    return shuffled[places]


def draw_row_subs(key, part):
    return make_lists(key)


def draw_station_subs(key, part):
    lists = make_lists(key)
    scores = jax.random.randint(jax.random.fold_in(key, 23), (STA, LS), 0, 1 << 20) * LS + jnp.arange(LS, dtype=jnp.int32)[None, :]
    order = jnp.argsort(-scores, axis=1)[:, :MS]
    owners = lists[jnp.arange(STA, dtype=jnp.int32) // ROW_STA]
    return jnp.take_along_axis(owners, order, axis=1).astype(jnp.int32)


def set_ends(drawn, rng, low, high):
    shape = drawn.shape
    index_at = [jax.random.randint(jax.random.fold_in(rng, axis), (), 0, shape[axis]) for axis in range(len(shape))]
    drawn = drawn.at[tuple(index_at)].set(low)
    longest = shape.index(max(shape))
    index_at[longest] = (index_at[longest] + 1) % shape[longest]
    return drawn.at[tuple(index_at)].set(high)


def steps_of(key, dims, cuts, least, largest):
    level, own = 1.0, jax.random.fold_in(key, 6)
    for position, blocks in cuts:
        heights = jnp.exp(jax.random.uniform(jax.random.fold_in(own, position), (blocks,), jnp.float32, least / len(cuts), largest / len(cuts)))
        level = level * jnp.repeat(heights, dims[position] // blocks).reshape([-1 if axis == position else 1 for axis in range(len(dims))])
    return level


def normal_values(rng, extent, spread, most, pieces=(), kind=jnp.bfloat16):
    drawn = jax.random.normal(rng, extent, jnp.float32) * spread
    if len(pieces) > 0:
        drawn = steps_of(rng, extent, pieces, -0.22, 0.18) * drawn
    return jnp.clip(drawn, min=-most, max=most).astype(kind)


def setup_inputs(seed: int = 0) -> dict:
    seeds = jax.random.split(jax.random.key(seed), 6)
    spectra = normal_values(seeds[0], (STA, F, WIN2), 1.0, 6.0, ((0, 128),))
    pair_bins = set_ends(jax.random.randint(seeds[1], (STA, STA), 0, NBIN), jax.random.fold_in(seeds[1], 1), 0, NBIN - 1).astype(jnp.int32)
    row_subs = draw_row_subs(jax.random.fold_in(seeds[5], 71), 0)
    station_subs = draw_station_subs(jax.random.fold_in(seeds[5], 71), 0)
    kernel = normal_values(seeds[4], (F, NBIN, V), NBIN ** -0.5, 0.375)
    return {"spectra": spectra, "pair_bins": pair_bins, "row_subs": row_subs, "station_subs": station_subs, "kernel": kernel}


def reference(spectra, pair_bins, row_subs, station_subs, kernel):
    stations = spectra.shape[0]
    shard_rows = stations // (N_ROW * N_COL)
    row_span = stations // N_ROW
    col_span = stations // N_COL
    slot_count = row_subs.shape[1]
    positions = jnp.arange(col_span, dtype=jnp.int32)
    bin_ids = jnp.arange(NBIN, dtype=jnp.int32)

    def one_block(running, block_index):
        row_block = block_index // N_COL
        col_group = block_index % N_COL
        row_first = (row_block * row_span).astype(jnp.int32)
        row_spectra = lax.dynamic_slice_in_dim(spectra, row_first, row_span, 0).astype(jnp.float32)
        col_ids = ((positions // shard_rows * N_COL + col_group) * shard_rows + positions % shard_rows).astype(jnp.int32)
        col_spectra = jnp.take(spectra, col_ids, axis=0).astype(jnp.float32)
        cross_spec = jnp.einsum('aft,jft->faj', row_spectra, col_spectra, precision=lax.Precision.HIGHEST)
        cross_spec = lax.optimization_barrier(cross_spec.astype(jnp.bfloat16)).astype(jnp.float32)
        bins_block = lax.dynamic_slice(pair_bins, (row_first, (col_group * col_span).astype(jnp.int32)), (row_span, col_span))
        slot_subs = lax.dynamic_index_in_dim(row_subs, row_block.astype(jnp.int32), 0, keepdims=False)
        row_members = lax.dynamic_slice_in_dim(station_subs, row_first, row_span, 0)
        col_members = jnp.take(station_subs, col_ids, axis=0)
        row_mask = jnp.any(row_members[None, :, :] == slot_subs[:, None, None], axis=2).astype(jnp.float32)
        col_mask = jnp.any(col_members[None, :, :] == slot_subs[:, None, None], axis=2).astype(jnp.float32)
        weighted = row_mask[:, None, :, None] * col_mask[:, None, None, :] * cross_spec[None]
        onehot = (bins_block.reshape(-1, 1) == bin_ids[None, :]).astype(jnp.float32)
        partial_value = jnp.dot(weighted.reshape(slot_count * F, row_span * col_span), onehot, precision=lax.Precision.HIGHEST)
        running = running.at[slot_subs].add(partial_value.reshape(slot_count, F, NBIN))
        return (running, None)
    start_sums = jnp.zeros((NSUB, F, NBIN), jnp.float32)
    binned_sum, unused = lax.scan(one_block, start_sums, jnp.arange(N_ROW * N_COL, dtype=jnp.int32))
    binned = lax.optimization_barrier(binned_sum.astype(jnp.bfloat16)).astype(jnp.float32)
    velocity_power = jnp.einsum('sfb,fbv->sfv', binned, kernel.astype(jnp.float32), precision=lax.Precision.HIGHEST)
    scale = lax.rsqrt(lax.optimization_barrier(jnp.mean(velocity_power * velocity_power, axis=2, keepdims=True)) + 1e-06)
    return velocity_power * scale
```

```python
import jax
import jax.numpy as jnp
from jax import lax
from jax.experimental import pallas as pl
from jax.experimental.pallas import tpu as pltpu
from jax.sharding import PartitionSpec as P

NZ, NCORE, NY, NX = 4, 2, 4, 4
F, FG, FP = 32, 8, 2
T = 128
NB, NI, NJ = 256, 256, 512
ST = 16
NS = 32
PJ, PS = 520, 40
UN = 8
NSUB = 128


def col_shift(v, dy, dx):
    pairs = []
    for y in range(NY):
        for x in range(NX):
            pairs.append((y * NX + x, (y + dy) % NY * NX + (x + dx) % NX))
    return lax.ppermute(v, "col", pairs)


def row_shift(v, dz, dcore):
    pairs = []
    for z in range(NZ):
        for k in range(NCORE):
            pairs.append((z * NCORE + k, (z + dz) % NZ * NCORE + (k + dcore) % NCORE))
    return lax.ppermute(v, "row", pairs)


def binning_kernel(list_ref, slots_ref, pos_ref, *refs):
    r_refs, c_refs, b_refs = refs[0:4], refs[4:12], refs[12:16]
    rowmask_ref = refs[16]
    outs = refs[17:21]
    R, C, XT, BN, RM, ACC = refs[21:27]
    x, y, z, core, n = [pos_ref[k] for k in range(5)]
    for yy in range(4):
        ys = lax.rem(y + (4 - yy), 4)
        for d in range(4):
            xs = lax.rem(x + (4 - d), 4)
            off = pl.multiple_of(ys * 64 + xs * 16, 16)
            R[:, pl.ds(off, ST), :] = r_refs[d][yy]
            zs = lax.rem(z + (4 - d), 4)
            for k in range(2):
                g = zs * 2 + (core if k == 0 else 1 - core)
                off = pl.multiple_of(ys * 128 + g * 16, 16)
                C[:, pl.ds(off, ST), :] = c_refs[k * 4 + d][yy]
        off = pl.multiple_of(ys * 128, 8)
        BN[pl.ds(off, 128), :] = b_refs[yy][...].astype(jnp.int32)
    for s in range(PS):
        RM[s] = jnp.broadcast_to(rowmask_ref[pl.ds(s, 1), :], (FG, NI))
    ACC[...] = jnp.zeros_like(ACC)
    for f in range(FG):
        v = lax.dot_general(
            C[f], R[f], (((1,), (1,)), ((), ())), preferred_element_type=jnp.float32
        )
        v = v.astype(jnp.bfloat16).astype(jnp.float32)
        for h in range(2):
            XT[(h * FG + f) * PJ : (h * FG + f) * PJ + NJ, :] = v[:, h * 128 : (h + 1) * 128]
    for row in range(NJ, PJ):
        BN[row : row + 1, :] = jnp.zeros((1, NI), jnp.int32)
    for hf in range(2 * FG):
        XT[hf * PJ + NJ : (hf + 1) * PJ, :] = jnp.zeros((PJ - NJ, 128), jnp.float32)
    iota = lax.broadcasted_iota(jnp.int32, (NB, NI), 0)

    def one(j):
        ss = [slots_ref[k, j] for k in range(8)]
        xv = jnp.concatenate(
            [XT[pl.ds(h * FG * PJ + j, FG, stride=PJ), :] for h in range(2)], axis=1
        )
        w = jnp.concatenate([xv * RM[s] for s in ss], axis=0).astype(jnp.bfloat16)
        pb = jnp.broadcast_to(BN[pl.ds(j, 1), :], (NB, NI))
        oh = jnp.where(pb == iota, 1.0, 0.0).astype(jnp.bfloat16)
        res = lax.dot_general(w, oh, (((1,), (1,)), ((), ())), preferred_element_type=jnp.float32)
        return ss, res

    def body(t, carry):
        done = [one(list_ref[t * UN + u]) for u in range(UN)]
        for ss, res in done:
            at = [[pl.ds(pl.multiple_of(h * PS * 8 + s * 8, 8), 8) for h in range(2)] for s in ss]
            old = [[ACC[at[k][h], :] for h in range(2)] for k in range(8)]
            for k in range(8):
                for h in range(2):
                    ACC[at[k][h], :] = (
                        old[k][h] + res[8 * k : 8 * k + 8, h * 128 : (h + 1) * 128]
                    )
        return carry

    lax.fori_loop(0, (n + UN - 1) // UN, body, 0)
    for d in range(4):
        xd = lax.rem(x + d, 4)
        for f in range(FP):
            for h in range(2):
                piece = ACC[pl.ds(h * PS * 8 + FP * xd + f, NS, stride=8), :]
                outs[d][f * NS : (f + 1) * NS, h * 128 : (h + 1) * 128] = piece.astype(
                    outs[d].dtype
                )


def whole(a):
    return pl.BlockSpec(a.shape, lambda i, *_: (0,) * a.ndim)


def binning(listed, slots, pos, rs, cs, bs, rowmask):
    arrays = [*rs, *cs, *bs, rowmask]
    outs = [jax.ShapeDtypeStruct((FP * NS, NB), jnp.float32)]
    outs += [jax.ShapeDtypeStruct((FP * NS, NB), jnp.bfloat16)] * 3
    return pl.pallas_call(
        binning_kernel,
        out_shape=outs,
        grid_spec=pltpu.PrefetchScalarGridSpec(
            num_scalar_prefetch=3,
            grid=(1,),
            in_specs=[whole(a) for a in arrays],
            out_specs=[whole(a) for a in outs],
            scratch_shapes=[
                pltpu.VMEM((FG, NI, T), jnp.bfloat16),
                pltpu.VMEM((FG, NJ, T), jnp.bfloat16),
                pltpu.VMEM((2 * FG * PJ, 128), jnp.float32),
                pltpu.VMEM((PJ, NI), jnp.int32),
                pltpu.VMEM((PS, FG, NI), jnp.float32),
                pltpu.VMEM((2 * PS * 8, 128), jnp.float32),
            ],
        ),
        compiler_params=pltpu.CompilerParams(vmem_limit_bytes=40 << 20),
        name="binning",
    )(listed, slots, pos, *arrays)


def project_kernel(pos_ref, *refs):
    g_refs, id_refs, kernel_ref, out_ref = refs[0:8], refs[8:12], refs[12], refs[13]
    y, x = pos_ref[1], pos_ref[0]
    first = (pos_ref[2] * 2 + pos_ref[3]) * 16
    wanted = first + lax.broadcasted_iota(jnp.int32, (16, NS), 0)
    picks = []
    for k in range(2):
        for d in range(4):
            ids = jnp.broadcast_to(id_refs[d][k : k + 1, :], (16, NS))
            picks.append(jnp.where(ids == wanted, 1.0, 0.0).astype(jnp.bfloat16))
    for f in range(FP):
        total = jnp.zeros((16, NB), jnp.float32)
        for p in range(8):
            total += jnp.dot(
                picks[p],
                g_refs[p][f * NS : (f + 1) * NS, :],
                preferred_element_type=jnp.float32,
            )
        power = jnp.dot(
            total.astype(jnp.bfloat16), kernel_ref[f], preferred_element_type=jnp.float32
        )
        scale = lax.rsqrt(jnp.mean(power * power, axis=1, keepdims=True) + 1e-06)
        out_ref[:, f * 256 : (f + 1) * 256] = power * scale


def project(pos, gs, ids, kernel):
    arrays = [*gs, *ids]
    out = jax.ShapeDtypeStruct((16, FP * 256), jnp.float32)
    return pl.pallas_call(
        project_kernel,
        out_shape=out,
        grid_spec=pltpu.PrefetchScalarGridSpec(
            num_scalar_prefetch=1,
            grid=(1,),
            in_specs=[whole(a) for a in arrays]
            + [pl.BlockSpec((FP, NB, 256), lambda i, pos: (pos[1] * 4 + pos[0], 0, 0))],
            out_specs=whole(out),
        ),
        name="project",
    )(pos, *arrays, kernel)


def on_device(spectra, pair_bins, row_subs, station_subs, kernel):
    row, col = lax.axis_index("row"), lax.axis_index("col")
    z, core, y, x = row // NCORE, row % NCORE, col // NX, col % NX

    by_freq = spectra.transpose(1, 0, 2).reshape(NY, FG, ST, T)
    own = [lax.dynamic_index_in_dim(by_freq, (y + d) % NY, 0, keepdims=False) for d in range(NY)]
    mine = jnp.stack([own[0]] + [col_shift(own[d], d, 0) for d in range(1, NY)])
    row_pieces = [mine] + [col_shift(mine, 0, d) for d in range(1, NX)]
    col_pieces = [mine] + [row_shift(mine, d, 0) for d in range(1, NZ)]
    col_pieces += [row_shift(p, 0, 1) for p in col_pieces]
    bins_t = pair_bins.astype(jnp.bfloat16).T
    bins_pieces = [bins_t] + [col_shift(bins_t, d, 0) for d in range(1, NY)]
    sub_ids = jnp.concatenate([row_subs, row_shift(row_subs, 0, 1)], axis=0)
    sub_pieces = [sub_ids] + [row_shift(sub_ids, d, 0) for d in range(1, NZ)]

    slot_subs = row_subs[0]
    row_members = lax.dynamic_slice_in_dim(station_subs, row * NI, NI, 0)
    rowmask = jnp.any(row_members[None] == slot_subs[:, None, None], axis=2)
    rowmask = jnp.pad(rowmask.astype(jnp.float32), ((0, PS - NS), (0, 0)))
    members = lax.dynamic_index_in_dim(
        station_subs.reshape(8, NY, NX, ST, 8), x, 2, keepdims=False
    )
    members = members.transpose(3, 1, 0, 2).reshape(8, NJ)
    hit = members[None] == slot_subs[:, None, None]
    slot_ids = jnp.arange(NS, dtype=jnp.int32) - NS
    slots = NS + jnp.sum(jnp.where(hit, slot_ids[:, None, None], 0), axis=0)
    used = jnp.any(slots < NS, axis=0)
    slots = jnp.pad(slots, ((0, 0), (0, PJ - NJ)), constant_values=NS)
    columns = jnp.arange(NJ, dtype=jnp.int32)
    before = jnp.sum((columns[:, None] < columns[None, :]) & used[:, None], axis=0)
    count = jnp.sum(used.astype(jnp.int32))
    places = jnp.arange(PJ, dtype=jnp.int32)
    at_place = used[:, None] & (before[:, None] == places[None, :])
    listed = NJ + jnp.sum(jnp.where(at_place, columns[:, None] - NJ, 0), axis=0)
    zero = jnp.zeros((), jnp.int32)
    pos = jnp.stack([x, y, z, core, count, zero, zero, zero]).astype(jnp.int32)

    sums = binning(listed, slots, pos, row_pieces, col_pieces, bins_pieces, rowmask)
    total = sums[0]
    for d in range(1, NX):
        total = total + col_shift(sums[d], 0, d).astype(jnp.float32)
    total = total.astype(jnp.bfloat16)
    totals = [total] + [row_shift(total, d, 0) for d in range(1, NZ)]
    totals += [row_shift(p, 0, 1) for p in totals]
    spectrum = project(pos, totals, sub_pieces, kernel)
    spectrum = lax.all_to_all(spectrum, "col", 0, 0, tiled=True)
    return spectrum.reshape(1, F, 256)


def solution(mesh):
    in_specs = (P(("row", "col"), None, None), P("row", "col"), P("row", None), P(), P())
    out_specs = P(("row", "col"), None, None)
    return jax.shard_map(
        on_device, mesh=mesh, in_specs=in_specs, out_specs=out_specs, check_vma=False
    )
```

```python
import jax
import jax.numpy as jnp
from jax import lax
from jax.experimental import pallas as pl
from jax.experimental.pallas import tpu as pltpu
from jax.sharding import PartitionSpec as P

NZ, NCORE, NY, NX = 4, 2, 4, 4
F, FG, FP = 32, 8, 2
T = 128
NB, NI, NJ = 256, 256, 512
ST = 16
NS = 32
PJ, PS = 520, 40
IDS = 16
ROWS = FP * NS + IDS
UN = 16


def col_shift(v, dy, dx):
    pairs = []
    for y in range(NY):
        for x in range(NX):
            pairs.append((y * NX + x, (y + dy) % NY * NX + (x + dx) % NX))
    return lax.ppermute(v, "col", pairs)


def row_shift(v, dz, dcore):
    pairs = []
    for z in range(NZ):
        for k in range(NCORE):
            pairs.append((z * NCORE + k, (z + dz) % NZ * NCORE + (k + dcore) % NCORE))
    return lax.ppermute(v, "row", pairs)


def pack_kernel(pos_ref, spectra_ref, bins_ref, *refs):
    outs, S = refs[0:4], refs[4]
    S[...] = spectra_ref[...].reshape(ST * F, T).astype(jnp.float32)
    bins = bins_ref[...].astype(jnp.bfloat16)
    for d in range(NY):
        first = lax.rem(pos_ref[1] + d, NY) * FG
        for f in range(FG):
            piece = S[pl.ds(first + f, ST, stride=F), :]
            outs[d][f * ST : (f + 1) * ST, :] = piece.astype(jnp.bfloat16)
        outs[d][FG * ST :, :] = bins


def pack(pos, spectra, pair_bins):
    outs = [jax.ShapeDtypeStruct((FG * ST + NI, T), jnp.bfloat16)] * NY
    return pl.pallas_call(
        pack_kernel,
        out_shape=outs,
        grid_spec=pltpu.PrefetchScalarGridSpec(
            num_scalar_prefetch=1,
            grid=(1,),
            in_specs=[whole(spectra), whole(pair_bins)],
            out_specs=[whole(a) for a in outs],
            scratch_shapes=[pltpu.VMEM((ST * F, T), jnp.float32)],
        ),
        name="pack",
    )(pos, spectra, pair_bins)


def binning_kernel(list_ref, slots_ref, pos_ref, *refs):
    r_refs, c_refs, b_refs = refs[0:4], refs[4:12], refs[12:16]
    rowmask_ref = refs[16]
    outs = refs[17:21]
    R, C, XT, BN, RM, ACC = refs[21:27]
    x, y, z, core = [pos_ref[k] for k in range(4)]
    n = list_ref[PJ - 1] - NJ
    for yy in range(4):
        ys = lax.rem(y + (4 - yy), 4)
        for d in range(4):
            xs = lax.rem(x + (4 - d), 4)
            off = pl.multiple_of(ys * 64 + xs * 16, 16)
            R[:, pl.ds(off, ST), :] = r_refs[d][yy]
            zs = lax.rem(z + (4 - d), 4)
            for k in range(2):
                g = zs * 2 + (core if k == 0 else 1 - core)
                off = pl.multiple_of(ys * 128 + g * 16, 16)
                C[:, pl.ds(off, ST), :] = c_refs[k * 4 + d][yy]
        off = pl.multiple_of(ys * 128, 8)
        bins = b_refs[yy][FG * ST :, :].astype(jnp.float32)
        BN[pl.ds(off, 128), :] = bins.T.astype(jnp.int32)
    for s in range(PS):
        RM[s] = jnp.broadcast_to(rowmask_ref[pl.ds(s, 1), :], (FG, NI))
    ACC[...] = jnp.zeros_like(ACC)
    for f in range(FG):
        v = lax.dot_general(
            C[f], R[f], (((1,), (1,)), ((), ())), preferred_element_type=jnp.float32
        )
        v = v.astype(jnp.bfloat16).astype(jnp.float32)
        for h in range(2):
            XT[(h * FG + f) * PJ : (h * FG + f) * PJ + NJ, :] = v[:, h * 128 : (h + 1) * 128]
    for row in range(NJ, PJ):
        BN[row : row + 1, :] = jnp.zeros((1, NI), jnp.int32)
    for hf in range(2 * FG):
        XT[hf * PJ + NJ : (hf + 1) * PJ, :] = jnp.zeros((PJ - NJ, 128), jnp.float32)
    iota = lax.broadcasted_iota(jnp.int32, (128, NI), 0)

    def one(j):
        ss = [slots_ref[k, j] for k in range(8)]
        xv = jnp.concatenate(
            [XT[pl.ds(h * FG * PJ + j, FG, stride=PJ), :] for h in range(2)], axis=1
        )
        pb = BN[pl.ds(j, 1), :]
        upper = jnp.where(jnp.broadcast_to(pb, (FG, NI)) >= 128, xv, 0.0)
        lower = xv - upper
        w = jnp.concatenate([v * RM[s] for s in ss for v in (lower, upper)], axis=0)
        low_bits = jnp.broadcast_to(lax.bitwise_and(pb, 127), (128, NI))
        oh = jnp.where(low_bits == iota, 1.0, 0.0).astype(jnp.bfloat16)
        res = lax.dot_general(
            w.astype(jnp.bfloat16),
            oh,
            (((1,), (1,)), ((), ())),
            preferred_element_type=jnp.float32,
        )
        return ss, res

    def body(t, carry):
        done = [one(list_ref[t * UN + u]) for u in range(UN)]
        for ss, res in done:
            at = [[pl.ds(pl.multiple_of(h * PS * 8 + s * 8, 8), 8) for h in range(2)] for s in ss]
            old = [[ACC[at[k][h], :] for h in range(2)] for k in range(8)]
            for k in range(8):
                for h in range(2):
                    first = 16 * k + 8 * h
                    ACC[at[k][h], :] = old[k][h] + res[first : first + 8, :]
        return carry

    lax.fori_loop(0, (n + UN - 1) // UN, body, 0)
    for d in range(4):
        xd = lax.rem(x + d, 4)
        for f in range(FP):
            for h in range(2):
                piece = ACC[pl.ds(h * PS * 8 + FP * xd + f, NS, stride=8), :]
                outs[d][f * NS : (f + 1) * NS, h * 128 : (h + 1) * 128] = piece.astype(
                    outs[d].dtype
                )
        ids = rowmask_ref[PS:, :]
        outs[d][FP * NS :, :] = ids if d == 0 else jnp.zeros(ids.shape, outs[d].dtype)


def whole(a):
    return pl.BlockSpec(a.shape, lambda i, *_: (0,) * a.ndim)


def binning(listed, slots, pos, rs, cs, bs, rowmask):
    arrays = [*rs, *cs, *bs, rowmask]
    outs = [jax.ShapeDtypeStruct((ROWS, NB), jnp.float32)]
    outs += [jax.ShapeDtypeStruct((ROWS, NB), jnp.bfloat16)] * 3
    return pl.pallas_call(
        binning_kernel,
        out_shape=outs,
        grid_spec=pltpu.PrefetchScalarGridSpec(
            num_scalar_prefetch=3,
            grid=(1,),
            in_specs=[whole(a) for a in arrays],
            out_specs=[whole(a) for a in outs],
            scratch_shapes=[
                pltpu.VMEM((FG, NI, T), jnp.bfloat16),
                pltpu.VMEM((FG, NJ, T), jnp.bfloat16),
                pltpu.VMEM((2 * FG * PJ, 128), jnp.float32),
                pltpu.VMEM((PJ, NI), jnp.int32),
                pltpu.VMEM((PS, FG, NI), jnp.float32),
                pltpu.VMEM((2 * PS * 8, 128), jnp.float32),
            ],
        ),
        compiler_params=pltpu.CompilerParams(vmem_limit_bytes=40 << 20),
        name="binning",
    )(listed, slots, pos, *arrays)


def project_kernel(pos_ref, *refs):
    g_refs, kernel_ref, out_ref = refs[0:8], refs[8], refs[9]
    first = (pos_ref[2] * 2 + pos_ref[3]) * 16
    wanted = (first + lax.broadcasted_iota(jnp.int32, (16, NS), 0)).astype(jnp.float32)
    picks = []
    for p in range(8):
        ids = g_refs[p][FP * NS :, :].astype(jnp.float32)[0:1, 0:NS]
        ids = jnp.broadcast_to(ids, (16, NS))
        picks.append(jnp.where(ids == wanted, 1.0, 0.0).astype(jnp.bfloat16))
    for f in range(FP):
        total = jnp.zeros((16, NB), jnp.float32)
        for p in range(8):
            total += jnp.dot(
                picks[p],
                g_refs[p][f * NS : (f + 1) * NS, :],
                preferred_element_type=jnp.float32,
            )
        power = jnp.dot(
            total.astype(jnp.bfloat16), kernel_ref[f], preferred_element_type=jnp.float32
        )
        scale = lax.rsqrt(jnp.mean(power * power, axis=1, keepdims=True) + 1e-06)
        out_ref[:, f * 256 : (f + 1) * 256] = power * scale


def project(pos, gs, kernel):
    arrays = list(gs)
    out = jax.ShapeDtypeStruct((16, FP * 256), jnp.float32)
    return pl.pallas_call(
        project_kernel,
        out_shape=out,
        grid_spec=pltpu.PrefetchScalarGridSpec(
            num_scalar_prefetch=1,
            grid=(1,),
            in_specs=[whole(a) for a in arrays]
            + [pl.BlockSpec((FP, NB, 256), lambda i, pos: (pos[1] * 4 + pos[0], 0, 0))],
            out_specs=whole(out),
        ),
        name="project",
    )(pos, *arrays, kernel)


def on_device(spectra, pair_bins, row_subs, station_subs, kernel):
    row, col = lax.axis_index("row"), lax.axis_index("col")
    z, core, y, x = row // NCORE, row % NCORE, col // NX, col % NX

    pos_at = jnp.arange(8, dtype=jnp.int32)
    pos = jnp.where(pos_at == 0, x, jnp.where(pos_at == 1, y, jnp.where(pos_at == 2, z, core)))
    pos = pos.astype(jnp.int32)

    packed = pack(pos, spectra, pair_bins)
    packed = [packed[0]] + [col_shift(packed[d], d, 0) for d in range(1, NY)]

    slot_subs = row_subs[0]
    row_members = lax.dynamic_slice_in_dim(station_subs, row * NI, NI, 0)
    rowmask = jnp.any(row_members[None] == slot_subs[:, None, None], axis=2)
    rowmask = jnp.pad(rowmask.astype(jnp.float32), ((0, PS - NS + IDS), (0, 0)))
    rowmask = rowmask.at[PS, :NS].set(slot_subs.astype(jnp.float32))
    members = lax.dynamic_index_in_dim(
        station_subs.reshape(8, NY, NX, ST, 8), x, 2, keepdims=False
    )
    members = members.transpose(3, 1, 0, 2).reshape(8, NJ)
    hit = members[None] == slot_subs[:, None, None]
    slot_ids = jnp.arange(NS, dtype=jnp.int32) - NS
    slots = NS + jnp.sum(jnp.where(hit, slot_ids[:, None, None], 0), axis=0)
    used = jnp.any(slots < NS, axis=0)
    slots = jnp.pad(slots, ((0, 0), (0, PJ - NJ)), constant_values=NS)
    columns = jnp.arange(NJ, dtype=jnp.int32)
    before = jnp.sum((columns[:, None] < columns[None, :]) & used[:, None], axis=0)
    places = jnp.arange(PJ, dtype=jnp.int32)
    at_place = used[:, None] & (before[:, None] == places[None, :])
    entries = jnp.where(at_place, columns[:, None] - NJ, 0)
    entries = jnp.where(places[None, :] == PJ - 1, used[:, None].astype(jnp.int32), entries)
    listed = NJ + jnp.sum(entries, axis=0)

    mine = jnp.stack([p[: FG * ST].reshape(FG, ST, T) for p in packed])
    mine, listed, slots, rowmask = lax.optimization_barrier((mine, listed, slots, rowmask))
    row_pieces = [mine] + [col_shift(mine, 0, d) for d in range(1, NX)]
    col_pieces = [mine] + [row_shift(mine, d, 0) for d in range(1, NZ)]
    col_pieces += [row_shift(p, 0, 1) for p in col_pieces]

    sums = binning(listed, slots, pos, row_pieces, col_pieces, packed, rowmask)
    total = sums[0]
    for d in range(1, NX):
        total = total + col_shift(sums[d], 0, d).astype(jnp.float32)
    total = total.astype(jnp.bfloat16)
    totals = [total] + [row_shift(total, d, 0) for d in range(1, NZ)]
    totals += [row_shift(p, 0, 1) for p in totals]
    spectrum = project(pos, totals, kernel)
    spectrum = lax.all_to_all(spectrum, "col", 0, 0, tiled=True)
    return spectrum.reshape(1, F, 256)


def solution(mesh):
    in_specs = (P(("row", "col"), None, None), P("row", "col"), P("row", None), P(), P())
    out_specs = P(("row", "col"), None, None)
    return jax.shard_map(
        on_device, mesh=mesh, in_specs=in_specs, out_specs=out_specs, check_vma=False
    )
```

```python
import jax
import jax.numpy as jnp
from jax import lax
from jax.experimental import pallas as pl
from jax.experimental.pallas import tpu as pltpu
from jax.sharding import PartitionSpec as P

VMEM = pl.BlockSpec(memory_space=pltpu.VMEM)
AXES = ("z", "core", "y", "x")
NZ, NCORE, NY, NX = 4, 2, 4, 4
F, FG = 32, 8
T = 128
NB, NI, NJ = 256, 256, 512
ST = 16
NSUB = 128
PJ, PS = 520, 136
UN = 16


def shift(v, axis, d):
    n = lax.axis_size(axis)
    return lax.ppermute(v, axis, [(i, (i + d) % n) for i in range(n)])


def pack_kernel(spectra_ref, bins_ref, *refs):
    outs, S = refs[0:4], refs[4]
    y = lax.axis_index("y")
    S[...] = spectra_ref[...].reshape(ST * F, T).astype(jnp.float32)
    bins = bins_ref[...].astype(jnp.bfloat16)
    for d in range(NY):
        first = lax.rem(y + d, NY) * FG
        for f in range(FG):
            piece = S[pl.ds(first + f, ST, stride=F), :]
            outs[d][f * ST : (f + 1) * ST, :] = piece.astype(jnp.bfloat16)
        outs[d][FG * ST :, :] = bins


def pack(spectra, pair_bins):
    outs = [jax.ShapeDtypeStruct((FG * ST + NI, T), jnp.bfloat16)] * NY
    return pl.pallas_call(
        pack_kernel,
        out_shape=outs,
        in_specs=[VMEM, VMEM],
        out_specs=[VMEM] * NY,
        scratch_shapes=[pltpu.VMEM((ST * F, T), jnp.float32)],
        name="pack",
    )(spectra, pair_bins)


def binning_kernel(list_ref, slots_ref, *refs):
    r_refs, c_refs, b_refs = refs[0:4], refs[4:12], refs[12:16]
    rowmask_ref = refs[16]
    outs = refs[17:21]
    R, C, XT, BN, RM, ACC = refs[21:27]
    z, core, y, x = [lax.axis_index(a) for a in AXES]
    n = list_ref[PJ - 1] - NJ
    for yy in range(4):
        ys = lax.rem(y + (4 - yy), 4)
        for d in range(4):
            xs = lax.rem(x + (4 - d), 4)
            off = pl.multiple_of(ys * 64 + xs * 16, 16)
            R[:, pl.ds(off, ST), :] = r_refs[d][yy]
            zs = lax.rem(z + (4 - d), 4)
            for k in range(2):
                g = zs * 2 + (core if k == 0 else 1 - core)
                off = pl.multiple_of(ys * 128 + g * 16, 16)
                C[:, pl.ds(off, ST), :] = c_refs[k * 4 + d][yy]
        off = pl.multiple_of(ys * 128, 8)
        bins = b_refs[yy][FG * ST :, :].astype(jnp.float32)
        BN[pl.ds(off, 128), :] = bins.T.astype(jnp.int32)
    for s in range(PS):
        RM[s] = jnp.broadcast_to(rowmask_ref[pl.ds(s, 1), :], (FG, NI))
    ACC[...] = jnp.zeros_like(ACC)
    for f in range(FG):
        v = lax.dot_general(
            C[f], R[f], (((1,), (1,)), ((), ())), preferred_element_type=jnp.float32
        )
        v = v.astype(jnp.bfloat16).astype(jnp.float32)
        for h in range(2):
            XT[(h * FG + f) * PJ : (h * FG + f) * PJ + NJ, :] = v[:, h * 128 : (h + 1) * 128]
    for row in range(NJ, PJ):
        BN[row : row + 1, :] = jnp.zeros((1, NI), jnp.int32)
    for hf in range(2 * FG):
        XT[hf * PJ + NJ : (hf + 1) * PJ, :] = jnp.zeros((PJ - NJ, 128), jnp.float32)
    iota = lax.broadcasted_iota(jnp.int32, (128, NI), 0)

    def one(j):
        ss = [slots_ref[k, j] for k in range(8)]
        xv = jnp.concatenate(
            [XT[pl.ds(h * FG * PJ + j, FG, stride=PJ), :] for h in range(2)], axis=1
        )
        pb = BN[pl.ds(j, 1), :]
        upper = jnp.where(jnp.broadcast_to(pb, (FG, NI)) >= 128, xv, 0.0)
        lower = xv - upper
        w = jnp.concatenate([v * RM[s] for s in ss for v in (lower, upper)], axis=0)
        low_bits = jnp.broadcast_to(lax.bitwise_and(pb, 127), (128, NI))
        oh = jnp.where(low_bits == iota, 1.0, 0.0).astype(jnp.bfloat16)
        res = lax.dot_general(
            w.astype(jnp.bfloat16),
            oh,
            (((1,), (1,)), ((), ())),
            preferred_element_type=jnp.float32,
        )
        return ss, res

    def body(t, carry):
        done = [one(list_ref[t * UN + u]) for u in range(UN)]
        for ss, res in done:
            at = [[pl.ds(pl.multiple_of(h * PS * 8 + s * 8, 8), 8) for h in range(2)] for s in ss]
            old = [[ACC[at[k][h], :] for h in range(2)] for k in range(8)]
            for k in range(8):
                for h in range(2):
                    first = 16 * k + 8 * h
                    ACC[at[k][h], :] = old[k][h] + res[first : first + 8, :]
        return carry

    lax.fori_loop(0, (n + UN - 1) // UN, body, 0)
    for d in range(4):
        xd = lax.rem(x + d, 4)
        for h in range(2):
            first = pl.multiple_of(h * PS * 8 + xd * 256, 8)
            piece = ACC[pl.ds(first, 256), :]
            outs[d][:, h * 128 : (h + 1) * 128] = piece.astype(outs[d].dtype)


def binning(listed, slots, rs, cs, bs, rowmask):
    arrays = [*rs, *cs, *bs, rowmask]
    outs = [jax.ShapeDtypeStruct((256, NB), jnp.float32)]
    outs += [jax.ShapeDtypeStruct((256, NB), jnp.bfloat16)] * 3
    return pl.pallas_call(
        binning_kernel,
        out_shape=outs,
        grid_spec=pltpu.PrefetchScalarGridSpec(
            num_scalar_prefetch=2,
            grid=(1,),
            in_specs=[VMEM] * len(arrays),
            out_specs=[VMEM] * len(outs),
            scratch_shapes=[
                pltpu.VMEM((FG, NI, T), jnp.bfloat16),
                pltpu.VMEM((FG, NJ, T), jnp.bfloat16),
                pltpu.VMEM((2 * FG * PJ, 128), jnp.float32),
                pltpu.VMEM((PJ, NI), jnp.int32),
                pltpu.VMEM((PS, FG, NI), jnp.float32),
                pltpu.VMEM((2 * PS * 8, 128), jnp.float32),
            ],
        ),
        compiler_params=pltpu.CompilerParams(vmem_limit_bytes=16 << 20),
        name="binning",
    )(listed, slots, *arrays)


def sum_kernel(own_ref, *refs):
    q_refs, mine_ref, other_ref = refs[0:3], refs[3], refs[4]
    core = lax.axis_index("core")
    for z in range(NZ):
        for out_ref, k in ((mine_ref, core), (other_ref, 1 - core)):
            rows = pl.ds(pl.multiple_of((z * 2 + k) * 32, 32), 32)
            total = own_ref[rows, :]
            for q_ref in q_refs:
                total = total + q_ref[rows, :].astype(jnp.float32)
            out_ref[z * 32 : (z + 1) * 32, :] = total


def sum_over_x(own, received):
    arrays = [own, *received]
    outs = [jax.ShapeDtypeStruct((128, NB), jnp.float32)] * 2
    return pl.pallas_call(
        sum_kernel,
        out_shape=outs,
        in_specs=[VMEM] * 4,
        out_specs=[VMEM] * 2,
        compiler_params=pltpu.CompilerParams(vmem_limit_bytes=4 << 20),
        name="sum_over_x",
    )(*arrays)


def project_kernel(sums_ref, kernel_ref, out_ref):
    total = jnp.zeros((F, NB), jnp.float32)
    for z in range(NZ):
        total = total + sums_ref[z * F : (z + 1) * F, :].astype(jnp.float32)
    binned = total.astype(jnp.bfloat16)
    row = lax.broadcasted_iota(jnp.int32, (16, 256), 0)
    for block in range(F // 16):
        power = jnp.zeros((16, 256), jnp.float32)
        for f in range(16):
            each = jnp.dot(
                binned[block * 16 : (block + 1) * 16, :],
                kernel_ref[block * 16 + f],
                preferred_element_type=jnp.float32,
            )
            power = jnp.where(row == f, each, power)
        scale = lax.rsqrt(jnp.mean(power * power, axis=1, keepdims=True) + 1e-06)
        out_ref[0, block * 16 : (block + 1) * 16, :] = power * scale


def project(sums, kernel):
    return pl.pallas_call(
        project_kernel,
        out_shape=jax.ShapeDtypeStruct((1, F, 256), jnp.float32),
        in_specs=[VMEM, VMEM],
        out_specs=VMEM,
        compiler_params=pltpu.CompilerParams(vmem_limit_bytes=4 << 20),
        name="project",
    )(sums, kernel)


def prefetch_kernel(kernel_ref, out_ref, done):
    copy = pltpu.make_async_copy(kernel_ref, out_ref, done)
    copy.start()
    copy.wait()


def prefetch(kernel):
    return pl.pallas_call(
        prefetch_kernel,
        out_shape=jax.ShapeDtypeStruct(kernel.shape, kernel.dtype),
        in_specs=[pl.BlockSpec(memory_space=pl.ANY)],
        out_specs=VMEM,
        scratch_shapes=[pltpu.SemaphoreType.DMA],
        compiler_params=pltpu.CompilerParams(vmem_limit_bytes=4 << 20),
        cost_estimate=pl.CostEstimate(
            flops=0, bytes_accessed=2 * kernel.size * 2, transcendentals=0
        ),
        name="prefetch",
    )(kernel)


def on_device(spectra, pair_bins, row_subs, station_subs, kernel):
    z, core, y, x = [lax.axis_index(a) for a in AXES]
    row = z * NCORE + core

    packed = pack(spectra, pair_bins)
    packed = [packed[0]] + [shift(packed[d], "y", d) for d in range(1, NY)]

    subs = jnp.arange(PS, dtype=jnp.int32)
    sub_at = (subs % 32 // 4) * 16 + subs % 4 * 4 + subs // 32
    slot_subs = row_subs[0]
    row_members = lax.dynamic_slice_in_dim(station_subs.T, row * NI, NI, 1)
    rowmask = jnp.any(row_members[None] == sub_at[:, None, None], axis=1)
    rowmask = jnp.where(subs[:, None] < NSUB, rowmask.astype(jnp.float32), 0.0)
    members = lax.dynamic_index_in_dim(
        station_subs.reshape(8, NY, NX, ST, 8), x, 2, keepdims=False
    )
    members = members.transpose(3, 1, 0, 2).reshape(8, NJ)
    hit = jnp.any(members[None] == slot_subs[:, None, None], axis=0)
    place = members % 4 * 32 + members // 16 * 4 + members // 4 % 4
    slots = jnp.where(hit, place, NSUB)
    used = jnp.any(hit, axis=0)
    slots = jnp.pad(slots, ((0, 0), (0, PJ - NJ)), constant_values=NSUB)
    columns = jnp.arange(NJ, dtype=jnp.int32)
    before = jnp.sum((columns[:, None] < columns[None, :]) & used[:, None], axis=0)
    places = jnp.arange(PJ, dtype=jnp.int32)
    at_place = used[:, None] & (before[:, None] == places[None, :])
    entries = jnp.where(at_place, columns[:, None] - NJ, 0)
    entries = jnp.where(places[None, :] == PJ - 1, used[:, None].astype(jnp.int32), entries)
    listed = NJ + jnp.sum(entries, axis=0)

    mine = jnp.stack([p[: FG * ST].reshape(FG, ST, T) for p in packed])
    mine, listed, slots, rowmask = lax.optimization_barrier((mine, listed, slots, rowmask))
    row_pieces = [mine] + [shift(mine, "x", d) for d in range(1, NX)]
    col_pieces = [mine] + [shift(mine, "z", d) for d in range(1, NZ)]
    col_pieces += [shift(p, "core", 1) for p in col_pieces]

    sums = binning(listed, slots, row_pieces, col_pieces, packed, rowmask)
    *sums, kernel = lax.optimization_barrier((*sums, kernel))
    kernel = prefetch(kernel)
    received = [shift(sums[d], "x", d) for d in range(1, NX)]
    kernel, *received = lax.optimization_barrier((kernel, *received))
    kept, passed = sum_over_x(sums[0], received)
    both = (kept + shift(passed, "core", 1)).astype(jnp.bfloat16)
    both = lax.all_to_all(both, ("z", "y"), 0, 0, tiled=True)
    return project(both, kernel)


def solution(mesh):
    chips = jax.sharding.Mesh(mesh.devices.reshape(NZ, NCORE, NY, NX), AXES)
    in_specs = (P(AXES, None, None), P(AXES[:2], AXES[2:]), P(AXES[:2], None), P(), P())
    out_specs = P(AXES, None, None)
    return jax.shard_map(
        on_device, mesh=chips, in_specs=in_specs, out_specs=out_specs, check_vma=False
    )
```

```python
import jax
import jax.numpy as jnp
from jax import lax
from jax.experimental import pallas as pl
from jax.experimental.pallas import tpu as pltpu
from jax.sharding import PartitionSpec as P

VMEM = pl.BlockSpec(memory_space=pltpu.VMEM)
AXES = ("z", "core", "y", "x")
NZ, NCORE, NY, NX = 4, 2, 4, 4
F, FG = 32, 8
T = 128
NB, NI, NJ = 256, 256, 512
ST = 16
NSUB = 128
PJ, PS = 520, 136
UN = 16


def shift(v, axis, d):
    n = lax.axis_size(axis)
    return lax.ppermute(v, axis, [(i, (i + d) % n) for i in range(n)])


def pack_kernel(spectra_ref, bins_ref, *refs):
    outs, S = refs[0:4], refs[4]
    y = lax.axis_index("y")
    S[...] = spectra_ref[...].reshape(ST * F, T).astype(jnp.float32)
    bins = bins_ref[...].astype(jnp.bfloat16)
    for d in range(NY):
        first = lax.rem(y + d, NY) * FG
        for f in range(FG):
            piece = S[pl.ds(first + f, ST, stride=F), :]
            outs[d][f * ST : (f + 1) * ST, :] = piece.astype(jnp.bfloat16)
        outs[d][FG * ST :, :] = bins


def pack(spectra, pair_bins):
    outs = [jax.ShapeDtypeStruct((FG * ST + NI, T), jnp.bfloat16)] * NY
    return pl.pallas_call(
        pack_kernel,
        out_shape=outs,
        in_specs=[VMEM, VMEM],
        out_specs=[VMEM] * NY,
        scratch_shapes=[pltpu.VMEM((ST * F, T), jnp.float32)],
        name="pack",
    )(spectra, pair_bins)


def binning_kernel(list_in, slots_in, *refs):
    r_refs, c_refs, b_refs = refs[0:4], refs[4:12], refs[12:16]
    rowmask_ref = refs[16]
    outs = refs[17:19]
    R, C, XT, BN, RM, ACC, list_ref, slots_ref, sems = refs[19:28]
    list_copy = pltpu.make_async_copy(list_in, list_ref, sems.at[0])
    slots_copy = pltpu.make_async_copy(slots_in, slots_ref, sems.at[1])
    list_copy.start()
    slots_copy.start()
    z, core, y, x = [lax.axis_index(a) for a in AXES]
    for yy in range(4):
        ys = lax.rem(y + (4 - yy), 4)
        for d in range(4):
            xs = lax.rem(x + (4 - d), 4)
            off = pl.multiple_of(ys * 64 + xs * 16, 16)
            R[:, pl.ds(off, ST), :] = r_refs[d][yy]
            zs = lax.rem(z + (4 - d), 4)
            for k in range(2):
                g = zs * 2 + (core if k == 0 else 1 - core)
                off = pl.multiple_of(ys * 128 + g * 16, 16)
                C[:, pl.ds(off, ST), :] = c_refs[k * 4 + d][yy]
        off = pl.multiple_of(ys * 128, 8)
        bins = b_refs[yy][FG * ST :, :].astype(jnp.float32)
        BN[pl.ds(off, 128), :] = bins.T.astype(jnp.int32)
    for s in range(PS):
        RM[s] = jnp.broadcast_to(rowmask_ref[pl.ds(s, 1), :], (FG, NI))
    ACC[...] = jnp.zeros_like(ACC)
    for f in range(FG):
        v = lax.dot_general(
            C[f], R[f], (((1,), (1,)), ((), ())), preferred_element_type=jnp.float32
        )
        v = v.astype(jnp.bfloat16).astype(jnp.float32)
        for h in range(2):
            XT[(h * FG + f) * PJ : (h * FG + f) * PJ + NJ, :] = v[:, h * 128 : (h + 1) * 128]
    for row in range(NJ, PJ):
        BN[row : row + 1, :] = jnp.zeros((1, NI), jnp.int32)
    for hf in range(2 * FG):
        XT[hf * PJ + NJ : (hf + 1) * PJ, :] = jnp.zeros((PJ - NJ, 128), jnp.float32)
    iota = lax.broadcasted_iota(jnp.int32, (128, NI), 0)

    def one(j, slots):
        ss = [slots_ref[k, j] for k in range(slots)]
        xv = jnp.concatenate(
            [XT[pl.ds(h * FG * PJ + j, FG, stride=PJ), :] for h in range(2)], axis=1
        )
        pb = BN[pl.ds(j, 1), :]
        upper = jnp.where(jnp.broadcast_to(pb, (FG, NI)) >= 128, xv, 0.0)
        lower = xv - upper
        w = jnp.concatenate([v * RM[s] for s in ss for v in (lower, upper)], axis=0)
        low_bits = jnp.broadcast_to(lax.bitwise_and(pb, 127), (128, NI))
        oh = jnp.where(low_bits == iota, 1.0, 0.0).astype(jnp.bfloat16)
        res = lax.dot_general(
            w.astype(jnp.bfloat16),
            oh,
            (((1,), (1,)), ((), ())),
            preferred_element_type=jnp.float32,
        )
        return ss, res

    def body(t, slots):
        done = [one(list_ref[0, t * UN + u], slots) for u in range(UN)]
        for ss, res in done:
            at = [[pl.ds(pl.multiple_of(h * PS * 8 + s * 8, 8), 8) for h in range(2)] for s in ss]
            old = [[ACC[at[k][h], :] for h in range(2)] for k in range(slots)]
            for k in range(slots):
                for h in range(2):
                    first = 16 * k + 8 * h
                    ACC[at[k][h], :] = old[k][h] + res[first : first + 8, :]

    list_copy.wait()
    slots_copy.wait()
    many = (list_ref[0, PJ - 2] - NJ + UN - 1) // UN
    total = (list_ref[0, PJ - 1] - NJ + UN - 1) // UN

    @pl.loop(0, many)
    def _(t):
        body(t, 8)

    @pl.loop(many, total)
    def _(t):
        body(t, 4)

    for d in range(4):
        xd = lax.rem(x + d, 4)
        for zd in range(NZ):
            for out_ref, k in ((outs[0], core), (outs[1], 1 - core)):
                for h in range(2):
                    first = pl.multiple_of(h * PS * 8 + xd * 256 + (zd * 2 + k) * 32, 8)
                    at = d * 128 + zd * 32
                    out_ref[at : at + 32, h * 128 : (h + 1) * 128] = ACC[pl.ds(first, 32), :]


def binning(listed, slots, rs, cs, bs, rowmask):
    arrays = [*rs, *cs, *bs, rowmask]
    outs = [jax.ShapeDtypeStruct((NX * 128, NB), jnp.float32)] * 2
    return pl.pallas_call(
        binning_kernel,
        out_shape=outs,
        in_specs=[VMEM] * (len(arrays) + 2),
        out_specs=[VMEM] * len(outs),
        scratch_shapes=[
            pltpu.VMEM((FG, NI, T), jnp.bfloat16),
            pltpu.VMEM((FG, NJ, T), jnp.bfloat16),
            pltpu.VMEM((2 * FG * PJ, 128), jnp.float32),
            pltpu.VMEM((PJ, NI), jnp.int32),
            pltpu.VMEM((PS, FG, NI), jnp.float32),
            pltpu.VMEM((2 * PS * 8, 128), jnp.float32),
            pltpu.SMEM((1, PJ), jnp.int32),
            pltpu.SMEM((8, PJ), jnp.int32),
            pltpu.SemaphoreType.DMA((2,)),
        ],
        compiler_params=pltpu.CompilerParams(vmem_limit_bytes=16 << 20),
        name="binning",
    )(listed, slots, *arrays)


def add_kernel(kept_ref, other_ref, *outs):
    for d in range(NX):
        rows = slice(d * 128, (d + 1) * 128)
        total = kept_ref[rows, :] + other_ref[rows, :]
        outs[d][...] = total.astype(outs[d].dtype)


def add_cores(kept, other):
    outs = [jax.ShapeDtypeStruct((128, NB), jnp.float32)]
    outs += [jax.ShapeDtypeStruct((128, NB), jnp.bfloat16)] * 3
    return pl.pallas_call(
        add_kernel,
        out_shape=outs,
        in_specs=[VMEM] * 2,
        out_specs=[VMEM] * NX,
        compiler_params=pltpu.CompilerParams(vmem_limit_bytes=4 << 20),
        name="add_cores",
    )(kept, other)


def project_kernel(sums_ref, kernel_ref, out_ref):
    total = jnp.zeros((F, NB), jnp.float32)
    for z in range(NZ):
        total = total + sums_ref[z * F : (z + 1) * F, :].astype(jnp.float32)
    binned = total.astype(jnp.bfloat16)
    row = lax.broadcasted_iota(jnp.int32, (16, 256), 0)
    for block in range(F // 16):
        power = jnp.zeros((16, 256), jnp.float32)
        for f in range(16):
            each = jnp.dot(
                binned[block * 16 : (block + 1) * 16, :],
                kernel_ref[block * 16 + f],
                preferred_element_type=jnp.float32,
            )
            power = jnp.where(row == f, each, power)
        scale = lax.rsqrt(jnp.mean(power * power, axis=1, keepdims=True) + 1e-06)
        out_ref[0, block * 16 : (block + 1) * 16, :] = power * scale


def project(sums, kernel):
    return pl.pallas_call(
        project_kernel,
        out_shape=jax.ShapeDtypeStruct((1, F, 256), jnp.float32),
        in_specs=[VMEM, VMEM],
        out_specs=VMEM,
        compiler_params=pltpu.CompilerParams(vmem_limit_bytes=4 << 20),
        name="project",
    )(sums, kernel)


def prefetch_kernel(kernel_ref, out_ref, done):
    copy = pltpu.make_async_copy(kernel_ref, out_ref, done)
    copy.start()
    copy.wait()


def prefetch(kernel):
    return pl.pallas_call(
        prefetch_kernel,
        out_shape=jax.ShapeDtypeStruct(kernel.shape, kernel.dtype),
        in_specs=[pl.BlockSpec(memory_space=pl.ANY)],
        out_specs=VMEM,
        scratch_shapes=[pltpu.SemaphoreType.DMA],
        compiler_params=pltpu.CompilerParams(vmem_limit_bytes=4 << 20),
        cost_estimate=pl.CostEstimate(
            flops=0, bytes_accessed=2 * kernel.size * 2, transcendentals=0
        ),
        name="prefetch",
    )(kernel)


def on_device(spectra, pair_bins, row_subs, station_subs, kernel):
    z, core, y, x = [lax.axis_index(a) for a in AXES]
    row = z * NCORE + core

    packed = pack(spectra, pair_bins)
    packed = [packed[0]] + [shift(packed[d], "y", d) for d in range(1, NY)]

    subs = jnp.arange(PS, dtype=jnp.int32)
    sub_at = (subs % 32 // 4) * 16 + subs % 4 * 4 + subs // 32
    slot_subs = row_subs[0]
    row_members = lax.dynamic_slice_in_dim(station_subs.T, row * NI, NI, 1)
    rowmask = jnp.any(row_members[None] == sub_at[:, None, None], axis=1)
    rowmask = jnp.where(subs[:, None] < NSUB, rowmask.astype(jnp.float32), 0.0)
    members = lax.dynamic_index_in_dim(
        station_subs.reshape(8, NY, NX, ST, 8), x, 2, keepdims=False
    )
    members = members.transpose(3, 1, 0, 2).reshape(8, NJ)
    hit = jnp.any(members[None] == slot_subs[:, None, None], axis=0)
    place = members % 4 * 32 + members // 16 * 4 + members // 4 % 4
    kth = jnp.arange(8, dtype=jnp.int32)
    rank = jnp.sum(hit[None] & (kth[None, :, None] < kth[:, None, None]), axis=1)
    at_rank = hit[None] & (rank[None] == kth[:, None, None])
    slots = NSUB + jnp.sum(jnp.where(at_rank, place[None] - NSUB, 0), axis=1)
    slots = jnp.pad(slots, ((0, 0), (0, PJ - NJ)), constant_values=NSUB)
    counts = jnp.sum(hit.astype(jnp.int32), axis=0)
    columns = jnp.arange(NJ, dtype=jnp.int32)
    used, many = counts > 0, counts > 4
    key = jnp.where(used, jnp.where(many, columns, columns + NJ), columns + 2 * NJ)
    before = jnp.sum(key[:, None] < key[None, :], axis=0)
    places = jnp.arange(PJ, dtype=jnp.int32)
    at_place = used[:, None] & (before[:, None] == places[None, :])
    entries = jnp.where(at_place, columns[:, None] - NJ, 0)
    entries = jnp.where(places[None, :] == PJ - 1, used[:, None].astype(jnp.int32), entries)
    entries = jnp.where(places[None, :] == PJ - 2, many[:, None].astype(jnp.int32), entries)
    listed = NJ + jnp.sum(entries, axis=0, keepdims=True)

    mine = jnp.stack([p[: FG * ST].reshape(FG, ST, T) for p in packed])
    mine, listed, slots, rowmask = lax.optimization_barrier((mine, listed, slots, rowmask))
    row_pieces = [mine] + [shift(mine, "x", d) for d in range(1, NX)]
    col_pieces = [mine] + [shift(mine, "z", d) for d in range(1, NZ)]
    col_pieces += [shift(p, "core", 1) for p in col_pieces]

    kept, passed = binning(listed, slots, row_pieces, col_pieces, packed, rowmask)
    own, *sums = add_cores(kept, shift(passed, "core", 1))
    *sums, kernel = lax.optimization_barrier((*sums, kernel))
    kernel = prefetch(kernel)
    received = [shift(sums[d - 1], "x", d) for d in range(1, NX)]
    kernel, *received = lax.optimization_barrier((kernel, *received))
    for part in received:
        own = own + part.astype(jnp.float32)
    both = lax.all_to_all(own.astype(jnp.bfloat16), ("z", "y"), 0, 0, tiled=True)
    return project(both, kernel)


def solution(mesh):
    chips = jax.sharding.Mesh(mesh.devices.reshape(NZ, NCORE, NY, NX), AXES)
    in_specs = (P(AXES, None, None), P(AXES[:2], AXES[2:]), P(AXES[:2], None), P(), P())
    out_specs = P(AXES, None, None)
    return jax.shard_map(
        on_device, mesh=chips, in_specs=in_specs, out_specs=out_specs, check_vma=False
    )
```

```python
import jax
import jax.numpy as jnp
from jax import lax
from jax.experimental import pallas as pl
from jax.experimental.pallas import tpu as pltpu
from jax.sharding import PartitionSpec as P

VMEM = pl.BlockSpec(memory_space=pltpu.VMEM)
AXES = ("z", "core", "y", "x")
NZ, NCORE, NY, NX = 4, 2, 4, 4
F, FG = 32, 8
T = 128
NB, NI, NJ = 256, 256, 512
ST = 16
NSUB = 128
PJ, PS = 520, 136
UN = 16


def shift(v, axis, d):
    n = lax.axis_size(axis)
    return lax.ppermute(v, axis, [(i, (i + d) % n) for i in range(n)])


def pack_kernel(spectra_ref, bins_ref, *refs):
    outs, S = refs[0:4], refs[4]
    y = lax.axis_index("y")
    S[...] = spectra_ref[...].reshape(ST * F, T).astype(jnp.float32)
    bins = bins_ref[...].astype(jnp.bfloat16)
    for d in range(NY):
        first = lax.rem(y + d, NY) * FG
        for f in range(FG):
            piece = S[pl.ds(first + f, ST, stride=F), :]
            outs[d][f * ST : (f + 1) * ST, :] = piece.astype(jnp.bfloat16)
        outs[d][FG * ST :, :] = bins


def pack(spectra, pair_bins):
    outs = [jax.ShapeDtypeStruct((FG * ST + NI, T), jnp.bfloat16)] * NY
    return pl.pallas_call(
        pack_kernel,
        out_shape=outs,
        in_specs=[VMEM, VMEM],
        out_specs=[VMEM] * NY,
        scratch_shapes=[pltpu.VMEM((ST * F, T), jnp.float32)],
        name="pack",
    )(spectra, pair_bins)


def tables_kernel(*refs):
    b_refs, rowmask_ref, BN, RM = refs[0:4], refs[4], refs[5], refs[6]
    y = lax.axis_index("y")
    for yy in range(NY):
        off = pl.multiple_of(lax.rem(y + (NY - yy), NY) * 128, 8)
        bins = b_refs[yy][FG * ST :, :].astype(jnp.float32)
        BN[pl.ds(off, 128), :] = bins.T.astype(jnp.int32)
    BN[NJ:PJ, :] = jnp.zeros((PJ - NJ, NI), jnp.int32)
    for s in range(PS):
        RM[s] = jnp.broadcast_to(rowmask_ref[pl.ds(s, 1), :], (2 * FG, NI)).astype(jnp.bfloat16)


def tables(bs, rowmask):
    return pl.pallas_call(
        tables_kernel,
        out_shape=[
            jax.ShapeDtypeStruct((PJ, NI), jnp.int32),
            jax.ShapeDtypeStruct((PS, 2 * FG, NI), jnp.bfloat16),
        ],
        in_specs=[VMEM] * 5,
        out_specs=[VMEM] * 2,
        compiler_params=pltpu.CompilerParams(vmem_limit_bytes=8 << 20),
        cost_estimate=pl.CostEstimate(flops=0, bytes_accessed=3 * 10**6, transcendentals=0),
        name="tables",
    )(*bs, rowmask)


def binning_kernel(list_in, slots_in, *refs):
    r_refs, c_refs, BN, RM = refs[0:4], refs[4:12], refs[12], refs[13]
    outs = refs[14:16]
    R, C, XT, ACC, list_ref, slots_ref, sems = refs[16:23]
    list_copy = pltpu.make_async_copy(list_in, list_ref, sems.at[0])
    slots_copy = pltpu.make_async_copy(slots_in, slots_ref, sems.at[1])
    list_copy.start()
    slots_copy.start()
    z, core, y, x = [lax.axis_index(a) for a in AXES]
    for yy in range(4):
        ys = lax.rem(y + (4 - yy), 4)
        for d in range(4):
            xs = lax.rem(x + (4 - d), 4)
            off = pl.multiple_of(ys * 64 + xs * 16, 16)
            R[:, pl.ds(off, ST), :] = r_refs[d][yy]
            zs = lax.rem(z + (4 - d), 4)
            for k in range(2):
                g = zs * 2 + (core if k == 0 else 1 - core)
                off = pl.multiple_of(ys * 128 + g * 16, 16)
                C[:, pl.ds(off, ST), :] = c_refs[k * 4 + d][yy]
    ACC[...] = jnp.zeros_like(ACC)
    for f in range(FG):
        v = lax.dot_general(
            C[f], R[f], (((1,), (1,)), ((), ())), preferred_element_type=jnp.float32
        )
        v = v.astype(jnp.bfloat16).astype(jnp.float32)
        for h in range(2):
            XT[(h * FG + f) * PJ : (h * FG + f) * PJ + NJ, :] = v[:, h * 128 : (h + 1) * 128]
    for hf in range(2 * FG):
        XT[hf * PJ + NJ : (hf + 1) * PJ, :] = jnp.zeros((PJ - NJ, 128), jnp.float32)
    iota = lax.broadcasted_iota(jnp.int32, (128, NI), 0)

    def one(j, slots):
        ss = [slots_ref[k, j] for k in range(slots)]
        xv = jnp.concatenate(
            [XT[pl.ds(h * FG * PJ + j, FG, stride=PJ), :] for h in range(2)], axis=1
        )
        pb = BN[pl.ds(j, 1), :]
        upper = jnp.where(jnp.broadcast_to(pb, (FG, NI)) >= 128, xv, 0.0)
        halves = jnp.concatenate([xv - upper, upper], axis=0).astype(jnp.bfloat16)
        w = jnp.concatenate([halves * RM[s] for s in ss], axis=0)
        low_bits = jnp.broadcast_to(lax.bitwise_and(pb, 127), (128, NI))
        oh = jnp.where(low_bits == iota, 1.0, 0.0).astype(jnp.bfloat16)
        res = lax.dot_general(
            w,
            oh,
            (((1,), (1,)), ((), ())),
            preferred_element_type=jnp.float32,
        )
        return ss, res

    def body(t, slots):
        done = [one(list_ref[0, t * UN + u], slots) for u in range(UN)]
        for ss, res in done:
            at = [[pl.ds(pl.multiple_of(h * PS * 8 + s * 8, 8), 8) for h in range(2)] for s in ss]
            old = [[ACC[at[k][h], :] for h in range(2)] for k in range(slots)]
            for k in range(slots):
                for h in range(2):
                    first = 16 * k + 8 * h
                    ACC[at[k][h], :] = old[k][h] + res[first : first + 8, :]

    list_copy.wait()
    slots_copy.wait()
    many = (list_ref[0, PJ - 2] - NJ + UN - 1) // UN
    total = (list_ref[0, PJ - 1] - NJ + UN - 1) // UN

    @pl.loop(0, many)
    def _(t):
        body(t, 8)

    @pl.loop(many, total)
    def _(t):
        body(t, 4)

    for d in range(4):
        xd = lax.rem(x + d, 4)
        for zd in range(NZ):
            for out_ref, k in ((outs[0], core), (outs[1], 1 - core)):
                for h in range(2):
                    first = pl.multiple_of(h * PS * 8 + xd * 256 + (zd * 2 + k) * 32, 8)
                    at = d * 128 + zd * 32
                    out_ref[at : at + 32, h * 128 : (h + 1) * 128] = ACC[pl.ds(first, 32), :]


def binning(listed, slots, rs, cs, BN, RM):
    arrays = [*rs, *cs, BN, RM]
    outs = [jax.ShapeDtypeStruct((NX * 128, NB), jnp.float32)] * 2
    return pl.pallas_call(
        binning_kernel,
        out_shape=outs,
        in_specs=[VMEM] * (len(arrays) + 2),
        out_specs=[VMEM] * len(outs),
        scratch_shapes=[
            pltpu.VMEM((FG, NI, T), jnp.bfloat16),
            pltpu.VMEM((FG, NJ, T), jnp.bfloat16),
            pltpu.VMEM((2 * FG * PJ, 128), jnp.float32),
            pltpu.VMEM((2 * PS * 8, 128), jnp.float32),
            pltpu.SMEM((1, PJ), jnp.int32),
            pltpu.SMEM((8, PJ), jnp.int32),
            pltpu.SemaphoreType.DMA((2,)),
        ],
        compiler_params=pltpu.CompilerParams(vmem_limit_bytes=16 << 20),
        name="binning",
    )(listed, slots, *arrays)


def add_kernel(kept_ref, other_ref, *outs):
    for d in range(NX):
        rows = slice(d * 128, (d + 1) * 128)
        total = kept_ref[rows, :] + other_ref[rows, :]
        outs[d][...] = total.astype(outs[d].dtype)


def add_cores(kept, other):
    outs = [jax.ShapeDtypeStruct((128, NB), jnp.float32)]
    outs += [jax.ShapeDtypeStruct((128, NB), jnp.bfloat16)] * 3
    return pl.pallas_call(
        add_kernel,
        out_shape=outs,
        in_specs=[VMEM] * 2,
        out_specs=[VMEM] * NX,
        compiler_params=pltpu.CompilerParams(vmem_limit_bytes=4 << 20),
        name="add_cores",
    )(kept, other)


def project_kernel(sums_ref, kernel_ref, out_ref):
    total = jnp.zeros((F, NB), jnp.float32)
    for z in range(NZ):
        total = total + sums_ref[z * F : (z + 1) * F, :].astype(jnp.float32)
    binned = total.astype(jnp.bfloat16)
    row = lax.broadcasted_iota(jnp.int32, (16, 256), 0)
    for block in range(F // 16):
        power = jnp.zeros((16, 256), jnp.float32)
        for f in range(16):
            each = jnp.dot(
                binned[block * 16 : (block + 1) * 16, :],
                kernel_ref[block * 16 + f],
                preferred_element_type=jnp.float32,
            )
            power = jnp.where(row == f, each, power)
        scale = lax.rsqrt(jnp.mean(power * power, axis=1, keepdims=True) + 1e-06)
        out_ref[0, block * 16 : (block + 1) * 16, :] = power * scale


def project(sums, kernel):
    return pl.pallas_call(
        project_kernel,
        out_shape=jax.ShapeDtypeStruct((1, F, 256), jnp.float32),
        in_specs=[VMEM, VMEM],
        out_specs=VMEM,
        compiler_params=pltpu.CompilerParams(vmem_limit_bytes=4 << 20),
        name="project",
    )(sums, kernel)


def prefetch_kernel(kernel_ref, out_ref, done):
    copy = pltpu.make_async_copy(kernel_ref, out_ref, done)
    copy.start()
    copy.wait()


def prefetch(kernel):
    return pl.pallas_call(
        prefetch_kernel,
        out_shape=jax.ShapeDtypeStruct(kernel.shape, kernel.dtype),
        in_specs=[pl.BlockSpec(memory_space=pl.ANY)],
        out_specs=VMEM,
        scratch_shapes=[pltpu.SemaphoreType.DMA],
        compiler_params=pltpu.CompilerParams(vmem_limit_bytes=4 << 20),
        cost_estimate=pl.CostEstimate(
            flops=0, bytes_accessed=2 * kernel.size * 2, transcendentals=0
        ),
        name="prefetch",
    )(kernel)


def on_device(spectra, pair_bins, row_subs, station_subs, kernel):
    z, core, y, x = [lax.axis_index(a) for a in AXES]
    row = z * NCORE + core

    packed = pack(spectra, pair_bins)
    packed = [packed[0]] + [shift(packed[d], "y", d) for d in range(1, NY)]

    subs = jnp.arange(PS, dtype=jnp.int32)
    sub_at = (subs % 32 // 4) * 16 + subs % 4 * 4 + subs // 32
    slot_subs = row_subs[0]
    row_members = lax.dynamic_slice_in_dim(station_subs.T, row * NI, NI, 1)
    rowmask = jnp.any(row_members[None] == sub_at[:, None, None], axis=1)
    rowmask = jnp.where(subs[:, None] < NSUB, rowmask.astype(jnp.float32), 0.0)
    members = lax.dynamic_index_in_dim(
        station_subs.reshape(8, NY, NX, ST, 8), x, 2, keepdims=False
    )
    members = members.transpose(3, 1, 0, 2).reshape(8, NJ)
    hit = jnp.any(members[None] == slot_subs[:, None, None], axis=0)
    place = members % 4 * 32 + members // 16 * 4 + members // 4 % 4
    kth = jnp.arange(8, dtype=jnp.int32)
    rank = jnp.sum(hit[None] & (kth[None, :, None] < kth[:, None, None]), axis=1)
    at_rank = hit[None] & (rank[None] == kth[:, None, None])
    slots = NSUB + jnp.sum(jnp.where(at_rank, place[None] - NSUB, 0), axis=1)
    slots = jnp.pad(slots, ((0, 0), (0, PJ - NJ)), constant_values=NSUB)
    counts = jnp.sum(hit.astype(jnp.int32), axis=0)
    columns = jnp.arange(NJ, dtype=jnp.int32)
    used, many = counts > 0, counts > 4
    key = jnp.where(used, jnp.where(many, columns, columns + NJ), columns + 2 * NJ)
    before = jnp.sum(key[:, None] < key[None, :], axis=0)
    places = jnp.arange(PJ, dtype=jnp.int32)
    at_place = used[:, None] & (before[:, None] == places[None, :])
    entries = jnp.where(at_place, columns[:, None] - NJ, 0)
    entries = jnp.where(places[None, :] == PJ - 1, used[:, None].astype(jnp.int32), entries)
    entries = jnp.where(places[None, :] == PJ - 2, many[:, None].astype(jnp.int32), entries)
    listed = NJ + jnp.sum(entries, axis=0, keepdims=True)

    mine = jnp.stack([p[: FG * ST].reshape(FG, ST, T) for p in packed])
    mine, listed, slots, rowmask = lax.optimization_barrier((mine, listed, slots, rowmask))
    row_pieces = [mine] + [shift(mine, "x", d) for d in range(1, NX)]
    col_pieces = [mine] + [shift(mine, "z", d) for d in range(1, NZ)]
    col_pieces += [shift(p, "core", 1) for p in col_pieces]

    row_pieces[2], rowmask = lax.optimization_barrier((row_pieces[2], rowmask))
    kept, passed = binning(listed, slots, row_pieces, col_pieces, *tables(packed, rowmask))
    own, *sums = add_cores(kept, shift(passed, "core", 1))
    *sums, kernel = lax.optimization_barrier((*sums, kernel))
    kernel = prefetch(kernel)
    received = [shift(sums[d - 1], "x", d) for d in range(1, NX)]
    kernel, *received = lax.optimization_barrier((kernel, *received))
    for part in received:
        own = own + part.astype(jnp.float32)
    both = lax.all_to_all(own.astype(jnp.bfloat16), ("z", "y"), 0, 0, tiled=True)
    return project(both, kernel)


def solution(mesh):
    chips = jax.sharding.Mesh(mesh.devices.reshape(NZ, NCORE, NY, NX), AXES)
    in_specs = (P(AXES, None, None), P(AXES[:2], AXES[2:]), P(AXES[:2], None), P(), P())
    out_specs = P(AXES, None, None)
    return jax.shard_map(
        on_device, mesh=chips, in_specs=in_specs, out_specs=out_specs, check_vma=False
    )
```

```python
import jax
import jax.numpy as jnp
from jax import lax
from jax.experimental import pallas as pl
from jax.experimental.pallas import tpu as pltpu
from jax.sharding import PartitionSpec as P

VMEM = pl.BlockSpec(memory_space=pltpu.VMEM)
AXES = ("z", "core", "y", "x")
NZ, NCORE, NY, NX = 4, 2, 4, 4
F, FG = 32, 8
T = 128
NB, NI, NJ = 256, 256, 512
ST = 16
NSUB = 128
PJ, PS = 520, 136
UN = 24
PL = 640


def shift(v, axis, d):
    n = lax.axis_size(axis)
    return lax.ppermute(v, axis, [(i, (i + d) % n) for i in range(n)])


def pack_kernel(spectra_ref, bins_ref, *refs):
    outs, S = refs[0:4], refs[4]
    y = lax.axis_index("y")
    S[...] = spectra_ref[...].reshape(ST * F, T).astype(jnp.float32)
    bins = bins_ref[...].astype(jnp.bfloat16)
    for d in range(NY):
        first = lax.rem(y + d, NY) * FG
        for f in range(FG):
            piece = S[pl.ds(first + f, ST, stride=F), :]
            outs[d][f * ST : (f + 1) * ST, :] = piece.astype(jnp.bfloat16)
        outs[d][FG * ST :, :] = bins


def pack(spectra, pair_bins):
    outs = [jax.ShapeDtypeStruct((FG * ST + NI, T), jnp.bfloat16)] * NY
    return pl.pallas_call(
        pack_kernel,
        out_shape=outs,
        in_specs=[VMEM, VMEM],
        out_specs=[VMEM] * NY,
        scratch_shapes=[pltpu.VMEM((ST * F, T), jnp.float32)],
        name="pack",
    )(spectra, pair_bins)


def tables_kernel(*refs):
    b_refs, rowmask_ref, BN, RM = refs[0:4], refs[4], refs[5], refs[6]
    y = lax.axis_index("y")
    for yy in range(NY):
        off = pl.multiple_of(lax.rem(y + (NY - yy), NY) * 128, 8)
        bins = b_refs[yy][FG * ST :, :].astype(jnp.float32)
        BN[pl.ds(off, 128), :] = bins.T.astype(jnp.int32)
    BN[NJ:PJ, :] = jnp.zeros((PJ - NJ, NI), jnp.int32)
    for s in range(PS):
        RM[s] = jnp.broadcast_to(rowmask_ref[pl.ds(s, 1), :], (2 * FG, NI)).astype(jnp.bfloat16)


def tables(bs, rowmask):
    return pl.pallas_call(
        tables_kernel,
        out_shape=[
            jax.ShapeDtypeStruct((PJ, NI), jnp.int32),
            jax.ShapeDtypeStruct((PS, 2 * FG, NI), jnp.bfloat16),
        ],
        in_specs=[VMEM] * 5,
        out_specs=[VMEM] * 2,
        compiler_params=pltpu.CompilerParams(vmem_limit_bytes=8 << 20),
        cost_estimate=pl.CostEstimate(flops=0, bytes_accessed=3 * 10**6, transcendentals=0),
        name="tables",
    )(*bs, rowmask)


def binning_kernel(list_in, slots_in, *refs):
    r_refs, c_refs, BN, RM = refs[0:4], refs[4:12], refs[12], refs[13]
    outs = refs[14:16]
    R, C, XT, ACC, list_ref, slots_ref, sems = refs[16:23]
    list_copy = pltpu.make_async_copy(list_in, list_ref, sems.at[0])
    slots_copy = pltpu.make_async_copy(slots_in, slots_ref, sems.at[1])
    list_copy.start()
    slots_copy.start()
    z, core, y, x = [lax.axis_index(a) for a in AXES]
    for yy in range(4):
        ys = lax.rem(y + (4 - yy), 4)
        for d in range(4):
            xs = lax.rem(x + (4 - d), 4)
            off = pl.multiple_of(ys * 64 + xs * 16, 16)
            R[:, pl.ds(off, ST), :] = r_refs[d][yy]
            zs = lax.rem(z + (4 - d), 4)
            for k in range(2):
                g = zs * 2 + (core if k == 0 else 1 - core)
                off = pl.multiple_of(ys * 128 + g * 16, 16)
                C[:, pl.ds(off, ST), :] = c_refs[k * 4 + d][yy]
    ACC[...] = jnp.zeros_like(ACC)
    for f in range(FG):
        v = lax.dot_general(
            C[f], R[f], (((1,), (1,)), ((), ())), preferred_element_type=jnp.float32
        )
        v = v.astype(jnp.bfloat16).astype(jnp.float32)
        for h in range(2):
            XT[(h * FG + f) * PJ : (h * FG + f) * PJ + NJ, :] = v[:, h * 128 : (h + 1) * 128]
    for hf in range(2 * FG):
        XT[hf * PJ + NJ : (hf + 1) * PJ, :] = jnp.zeros((PJ - NJ, 128), jnp.float32)
    iota = lax.broadcasted_iota(jnp.int32, (128, NI), 0)

    def one(j, slots):
        ss = [slots_ref[k, j] for k in range(slots)]
        xv = jnp.concatenate(
            [XT[pl.ds(h * FG * PJ + j, FG, stride=PJ), :] for h in range(2)], axis=1
        )
        pb = BN[pl.ds(j, 1), :]
        upper = jnp.where(jnp.broadcast_to(pb, (FG, NI)) >= 128, xv, 0.0)
        halves = jnp.concatenate([xv - upper, upper], axis=0).astype(jnp.bfloat16)
        w = jnp.concatenate([halves * RM[s] for s in ss], axis=0)
        low_bits = jnp.broadcast_to(lax.bitwise_and(pb, 127), (128, NI))
        oh = jnp.where(low_bits == iota, 1.0, 0.0).astype(jnp.bfloat16)
        res = lax.dot_general(
            w,
            oh,
            (((1,), (1,)), ((), ())),
            preferred_element_type=jnp.float32,
        )
        return ss, res

    def body(t, slots):
        done = [one(list_ref[0, t * UN + u], slots) for u in range(UN)]
        for ss, res in done:
            at = [[pl.ds(pl.multiple_of(h * PS * 8 + s * 8, 8), 8) for h in range(2)] for s in ss]
            old = [[ACC[at[k][h], :] for h in range(2)] for k in range(slots)]
            for k in range(slots):
                for h in range(2):
                    first = 16 * k + 8 * h
                    ACC[at[k][h], :] = old[k][h] + res[first : first + 8, :]

    list_copy.wait()
    slots_copy.wait()
    many = (list_ref[0, PL - 2] - NJ + UN - 1) // UN
    total = (list_ref[0, PL - 1] - NJ + UN - 1) // UN

    @pl.loop(0, many)
    def _(t):
        body(t, 8)

    @pl.loop(many, total)
    def _(t):
        body(t, 4)

    for d in range(4):
        xd = lax.rem(x + d, 4)
        for zd in range(NZ):
            for out_ref, k in ((outs[0], core), (outs[1], 1 - core)):
                for h in range(2):
                    first = pl.multiple_of(h * PS * 8 + xd * 256 + (zd * 2 + k) * 32, 8)
                    at = d * 128 + zd * 32
                    out_ref[at : at + 32, h * 128 : (h + 1) * 128] = ACC[pl.ds(first, 32), :]


def binning(listed, slots, rs, cs, BN, RM):
    arrays = [*rs, *cs, BN, RM]
    outs = [jax.ShapeDtypeStruct((NX * 128, NB), jnp.float32)] * 2
    return pl.pallas_call(
        binning_kernel,
        out_shape=outs,
        in_specs=[VMEM] * (len(arrays) + 2),
        out_specs=[VMEM] * len(outs),
        scratch_shapes=[
            pltpu.VMEM((FG, NI, T), jnp.bfloat16),
            pltpu.VMEM((FG, NJ, T), jnp.bfloat16),
            pltpu.VMEM((2 * FG * PJ, 128), jnp.float32),
            pltpu.VMEM((2 * PS * 8, 128), jnp.float32),
            pltpu.SMEM((1, PL), jnp.int32),
            pltpu.SMEM((8, PJ), jnp.int32),
            pltpu.SemaphoreType.DMA((2,)),
        ],
        compiler_params=pltpu.CompilerParams(vmem_limit_bytes=16 << 20),
        name="binning",
    )(listed, slots, *arrays)


def add_kernel(kept_ref, other_ref, *outs):
    for d in range(NX):
        rows = slice(d * 128, (d + 1) * 128)
        total = kept_ref[rows, :] + other_ref[rows, :]
        outs[d][...] = total.astype(outs[d].dtype)


def add_cores(kept, other):
    outs = [jax.ShapeDtypeStruct((128, NB), jnp.float32)]
    outs += [jax.ShapeDtypeStruct((128, NB), jnp.bfloat16)] * 3
    return pl.pallas_call(
        add_kernel,
        out_shape=outs,
        in_specs=[VMEM] * 2,
        out_specs=[VMEM] * NX,
        compiler_params=pltpu.CompilerParams(vmem_limit_bytes=4 << 20),
        name="add_cores",
    )(kept, other)


def project_kernel(sums_ref, kernel_ref, out_ref):
    total = jnp.zeros((F, NB), jnp.float32)
    for z in range(NZ):
        total = total + sums_ref[z * F : (z + 1) * F, :].astype(jnp.float32)
    binned = total.astype(jnp.bfloat16)
    row = lax.broadcasted_iota(jnp.int32, (16, 256), 0)
    for block in range(F // 16):
        power = jnp.zeros((16, 256), jnp.float32)
        for f in range(16):
            each = jnp.dot(
                binned[block * 16 : (block + 1) * 16, :],
                kernel_ref[block * 16 + f],
                preferred_element_type=jnp.float32,
            )
            power = jnp.where(row == f, each, power)
        scale = lax.rsqrt(jnp.mean(power * power, axis=1, keepdims=True) + 1e-06)
        out_ref[0, block * 16 : (block + 1) * 16, :] = power * scale


def project(sums, kernel):
    return pl.pallas_call(
        project_kernel,
        out_shape=jax.ShapeDtypeStruct((1, F, 256), jnp.float32),
        in_specs=[VMEM, VMEM],
        out_specs=VMEM,
        compiler_params=pltpu.CompilerParams(vmem_limit_bytes=4 << 20),
        name="project",
    )(sums, kernel)


def prefetch_kernel(kernel_ref, out_ref, done):
    copy = pltpu.make_async_copy(kernel_ref, out_ref, done)
    copy.start()
    copy.wait()


def prefetch(kernel):
    return pl.pallas_call(
        prefetch_kernel,
        out_shape=jax.ShapeDtypeStruct(kernel.shape, kernel.dtype),
        in_specs=[pl.BlockSpec(memory_space=pl.ANY)],
        out_specs=VMEM,
        scratch_shapes=[pltpu.SemaphoreType.DMA],
        compiler_params=pltpu.CompilerParams(vmem_limit_bytes=4 << 20),
        cost_estimate=pl.CostEstimate(
            flops=0, bytes_accessed=2 * kernel.size * 2, transcendentals=0
        ),
        name="prefetch",
    )(kernel)


def on_device(spectra, pair_bins, row_subs, station_subs, kernel):
    z, core, y, x = [lax.axis_index(a) for a in AXES]
    row = z * NCORE + core

    packed = pack(spectra, pair_bins)
    packed = [packed[0]] + [shift(packed[d], "y", d) for d in range(1, NY)]

    subs = jnp.arange(PS, dtype=jnp.int32)
    sub_at = (subs % 32 // 4) * 16 + subs % 4 * 4 + subs // 32
    slot_subs = row_subs[0]
    row_members = lax.dynamic_slice_in_dim(station_subs.T, row * NI, NI, 1)
    rowmask = jnp.any(row_members[None] == sub_at[:, None, None], axis=1)
    rowmask = jnp.where(subs[:, None] < NSUB, rowmask.astype(jnp.float32), 0.0)
    members = lax.dynamic_index_in_dim(
        station_subs.reshape(8, NY, NX, ST, 8), x, 2, keepdims=False
    )
    members = members.transpose(3, 1, 0, 2).reshape(8, NJ)
    hit = jnp.any(members[None] == slot_subs[:, None, None], axis=0)
    place = members % 4 * 32 + members // 16 * 4 + members // 4 % 4
    kth = jnp.arange(8, dtype=jnp.int32)
    rank = jnp.sum(hit[None] & (kth[None, :, None] < kth[:, None, None]), axis=1)
    at_rank = hit[None] & (rank[None] == kth[:, None, None])
    slots = NSUB + jnp.sum(jnp.where(at_rank, place[None] - NSUB, 0), axis=1)
    slots = jnp.pad(slots, ((0, 0), (0, PJ - NJ)), constant_values=NSUB)
    counts = jnp.sum(hit.astype(jnp.int32), axis=0)
    columns = jnp.arange(NJ, dtype=jnp.int32)
    used, many = counts > 0, counts > 4
    key = jnp.where(used, jnp.where(many, columns, columns + NJ), columns + 2 * NJ)
    before = jnp.sum(key[:, None] < key[None, :], axis=0)
    places = jnp.arange(PL, dtype=jnp.int32)
    at_place = used[:, None] & (before[:, None] == places[None, :])
    entries = jnp.where(at_place, columns[:, None] - NJ, 0)
    entries = jnp.where(places[None, :] == PL - 1, used[:, None].astype(jnp.int32), entries)
    entries = jnp.where(places[None, :] == PL - 2, many[:, None].astype(jnp.int32), entries)
    listed = NJ + jnp.sum(entries, axis=0, keepdims=True)

    mine = jnp.stack([p[: FG * ST].reshape(FG, ST, T) for p in packed])
    mine, listed, slots, rowmask = lax.optimization_barrier((mine, listed, slots, rowmask))
    row_pieces = [mine] + [shift(mine, "x", d) for d in range(1, NX)]
    col_pieces = [mine] + [shift(mine, "z", d) for d in range(1, NZ)]
    col_pieces += [shift(p, "core", 1) for p in col_pieces]

    row_pieces[2], rowmask = lax.optimization_barrier((row_pieces[2], rowmask))
    kept, passed = binning(listed, slots, row_pieces, col_pieces, *tables(packed, rowmask))
    own, *sums = add_cores(kept, shift(passed, "core", 1))
    *sums, kernel = lax.optimization_barrier((*sums, kernel))
    kernel = prefetch(kernel)
    received = [shift(sums[d - 1], "x", d) for d in range(1, NX)]
    kernel, *received = lax.optimization_barrier((kernel, *received))
    for part in received:
        own = own + part.astype(jnp.float32)
    both = lax.all_to_all(own.astype(jnp.bfloat16), ("z", "y"), 0, 0, tiled=True)
    return project(both, kernel)


def solution(mesh):
    chips = jax.sharding.Mesh(mesh.devices.reshape(NZ, NCORE, NY, NX), AXES)
    in_specs = (P(AXES, None, None), P(AXES[:2], AXES[2:]), P(AXES[:2], None), P(), P())
    out_specs = P(AXES, None, None)
    return jax.shard_map(
        on_device, mesh=chips, in_specs=in_specs, out_specs=out_specs, check_vma=False
    )
```

```python
import jax
import jax.numpy as jnp
from jax import lax
from jax.experimental import pallas as pl
from jax.experimental.pallas import tpu as pltpu
from jax.sharding import PartitionSpec as P

VMEM = pl.BlockSpec(memory_space=pltpu.VMEM)
AXES = ("z", "core", "y", "x")
NZ, NCORE, NY, NX = 4, 2, 4, 4
F, FG = 32, 8
T = 128
NB, NI, NJ = 256, 256, 512
ST = 16
NSUB = 128
PJ, PS = 520, 136
UN = 24
PL = 640


def shift(v, axis, d):
    n = lax.axis_size(axis)
    return lax.ppermute(v, axis, [(i, (i + d) % n) for i in range(n)])


def pack_kernel(spectra_ref, bins_ref, *refs):
    outs, S = refs[0:4], refs[4]
    y = lax.axis_index("y")
    S[...] = spectra_ref[...].reshape(ST * F, T).astype(jnp.float32)
    bins = bins_ref[...].astype(jnp.bfloat16)
    for d in range(NY):
        first = lax.rem(y + d, NY) * FG
        for f in range(FG):
            piece = S[pl.ds(first + f, ST, stride=F), :]
            outs[d][f * ST : (f + 1) * ST, :] = piece.astype(jnp.bfloat16)
        outs[d][FG * ST :, :] = bins


def pack(spectra, pair_bins):
    outs = [jax.ShapeDtypeStruct((FG * ST + NI, T), jnp.bfloat16)] * NY
    return pl.pallas_call(
        pack_kernel,
        out_shape=outs,
        in_specs=[VMEM, VMEM],
        out_specs=[VMEM] * NY,
        scratch_shapes=[pltpu.VMEM((ST * F, T), jnp.float32)],
        name="pack",
    )(spectra, pair_bins)


def tables_kernel(*refs):
    b_refs, rowmask_ref, BN, RM = refs[0:4], refs[4], refs[5], refs[6]
    y = lax.axis_index("y")
    for yy in range(NY):
        off = pl.multiple_of(lax.rem(y + (NY - yy), NY) * 128, 8)
        bins = b_refs[yy][FG * ST :, :].astype(jnp.float32)
        BN[pl.ds(off, 128), :] = bins.T.astype(jnp.int32)
    BN[NJ:PJ, :] = jnp.zeros((PJ - NJ, NI), jnp.int32)
    for s in range(PS):
        RM[s] = jnp.broadcast_to(rowmask_ref[pl.ds(s, 1), :], (2 * FG, NI)).astype(jnp.bfloat16)


def tables(bs, rowmask):
    return pl.pallas_call(
        tables_kernel,
        out_shape=[
            jax.ShapeDtypeStruct((PJ, NI), jnp.int32),
            jax.ShapeDtypeStruct((PS, 2 * FG, NI), jnp.bfloat16),
        ],
        in_specs=[VMEM] * 5,
        out_specs=[VMEM] * 2,
        compiler_params=pltpu.CompilerParams(vmem_limit_bytes=8 << 20),
        cost_estimate=pl.CostEstimate(flops=0, bytes_accessed=3 * 10**6, transcendentals=0),
        name="tables",
    )(*bs, rowmask)


def binning_kernel(list_in, slots_in, *refs):
    r_refs, c_refs, BN, RM = refs[0:4], refs[4:12], refs[12], refs[13]
    outs = refs[14:16]
    R, C, XT, ACC, list_ref, slots_ref, sems = refs[16:23]
    list_copy = pltpu.make_async_copy(list_in, list_ref, sems.at[0])
    slots_copy = pltpu.make_async_copy(slots_in, slots_ref, sems.at[1])
    list_copy.start()
    slots_copy.start()
    z, core, y, x = [lax.axis_index(a) for a in AXES]
    for yy in range(4):
        ys = lax.rem(y + (4 - yy), 4)
        for d in range(4):
            xs = lax.rem(x + (4 - d), 4)
            off = pl.multiple_of(ys * 64 + xs * 16, 16)
            R[:, pl.ds(off, ST), :] = r_refs[d][yy]
            zs = lax.rem(z + (4 - d), 4)
            for k in range(2):
                g = zs * 2 + (core if k == 0 else 1 - core)
                off = pl.multiple_of(ys * 128 + g * 16, 16)
                C[:, pl.ds(off, ST), :] = c_refs[k * 4 + d][yy]
    ACC[...] = jnp.zeros_like(ACC)
    for f in range(FG):
        v = lax.dot_general(
            C[f], R[f], (((1,), (1,)), ((), ())), preferred_element_type=jnp.float32
        )
        v = v.astype(jnp.bfloat16).astype(jnp.float32)
        for h in range(2):
            XT[(h * FG + f) * PJ : (h * FG + f) * PJ + NJ, :] = v[:, h * 128 : (h + 1) * 128]
    for hf in range(2 * FG):
        XT[hf * PJ + NJ : (hf + 1) * PJ, :] = jnp.zeros((PJ - NJ, 128), jnp.float32)
    iota = lax.broadcasted_iota(jnp.int32, (128, NI), 0)

    def one(j, slots):
        ss = [slots_ref[k, j] for k in range(slots)]
        xv = jnp.concatenate(
            [XT[pl.ds(h * FG * PJ + j, FG, stride=PJ), :] for h in range(2)], axis=1
        )
        pb = BN[pl.ds(j, 1), :]
        upper = jnp.where(jnp.broadcast_to(pb, (FG, NI)) >= 128, xv, 0.0)
        halves = jnp.concatenate([xv - upper, upper], axis=0).astype(jnp.bfloat16)
        w = jnp.concatenate([halves * RM[s] for s in ss], axis=0)
        low_bits = jnp.broadcast_to(lax.bitwise_and(pb, 127), (128, NI))
        oh = jnp.where(low_bits == iota, 1.0, 0.0).astype(jnp.bfloat16)
        res = lax.dot_general(
            w,
            oh,
            (((1,), (1,)), ((), ())),
            preferred_element_type=jnp.float32,
        )
        return ss, res

    def body(t, slots):
        done = [one(list_ref[0, t * UN + u], slots) for u in range(UN)]
        for ss, res in done:
            at = [[pl.ds(pl.multiple_of(h * PS * 8 + s * 8, 8), 8) for h in range(2)] for s in ss]
            old = [[ACC[at[k][h], :] for h in range(2)] for k in range(slots)]
            for k in range(slots):
                for h in range(2):
                    first = 16 * k + 8 * h
                    ACC[at[k][h], :] = old[k][h] + res[first : first + 8, :]

    list_copy.wait()
    slots_copy.wait()
    many = (list_ref[0, PL - 2] - NJ + UN - 1) // UN
    total = (list_ref[0, PL - 1] - NJ + UN - 1) // UN

    @pl.loop(0, many)
    def _(t):
        body(t, 8)

    @pl.loop(many, total)
    def _(t):
        body(t, 4)

    for d in range(4):
        xd = lax.rem(x + d, 4)
        for zd in range(NZ):
            for out_ref, k in ((outs[0], core), (outs[1], 1 - core)):
                for h in range(2):
                    first = pl.multiple_of(h * PS * 8 + xd * 256 + (zd * 2 + k) * 32, 8)
                    at = d * 128 + zd * 32
                    piece = ACC[pl.ds(first, 32), :].astype(out_ref.dtype)
                    out_ref[at : at + 32, h * 128 : (h + 1) * 128] = piece


def binning(listed, slots, rs, cs, BN, RM):
    arrays = [*rs, *cs, BN, RM]
    outs = [jax.ShapeDtypeStruct((NX * 128, NB), t) for t in (jnp.float32, jnp.bfloat16)]
    return pl.pallas_call(
        binning_kernel,
        out_shape=outs,
        in_specs=[VMEM] * (len(arrays) + 2),
        out_specs=[VMEM] * len(outs),
        scratch_shapes=[
            pltpu.VMEM((FG, NI, T), jnp.bfloat16),
            pltpu.VMEM((FG, NJ, T), jnp.bfloat16),
            pltpu.VMEM((2 * FG * PJ, 128), jnp.float32),
            pltpu.VMEM((2 * PS * 8, 128), jnp.float32),
            pltpu.SMEM((1, PL), jnp.int32),
            pltpu.SMEM((8, PJ), jnp.int32),
            pltpu.SemaphoreType.DMA((2,)),
        ],
        compiler_params=pltpu.CompilerParams(vmem_limit_bytes=16 << 20),
        name="binning",
    )(listed, slots, *arrays)


def add_kernel(kept_ref, other_ref, *outs):
    for d in range(NX):
        rows = slice(d * 128, (d + 1) * 128)
        total = kept_ref[rows, :] + other_ref[rows, :].astype(jnp.float32)
        outs[d][...] = total.astype(outs[d].dtype)


def add_cores(kept, other):
    outs = [jax.ShapeDtypeStruct((128, NB), jnp.float32)]
    outs += [jax.ShapeDtypeStruct((128, NB), jnp.bfloat16)] * 3
    return pl.pallas_call(
        add_kernel,
        out_shape=outs,
        in_specs=[VMEM] * 2,
        out_specs=[VMEM] * NX,
        compiler_params=pltpu.CompilerParams(vmem_limit_bytes=4 << 20),
        name="add_cores",
    )(kept, other)


def project_kernel(sums_ref, kernel_ref, out_ref):
    total = jnp.zeros((F, NB), jnp.float32)
    for z in range(NZ):
        total = total + sums_ref[z * F : (z + 1) * F, :].astype(jnp.float32)
    binned = total.astype(jnp.bfloat16)
    row = lax.broadcasted_iota(jnp.int32, (16, 256), 0)
    for block in range(F // 16):
        power = jnp.zeros((16, 256), jnp.float32)
        for f in range(16):
            each = jnp.dot(
                binned[block * 16 : (block + 1) * 16, :],
                kernel_ref[block * 16 + f],
                preferred_element_type=jnp.float32,
            )
            power = jnp.where(row == f, each, power)
        scale = lax.rsqrt(jnp.mean(power * power, axis=1, keepdims=True) + 1e-06)
        out_ref[0, block * 16 : (block + 1) * 16, :] = power * scale


def project(sums, kernel):
    return pl.pallas_call(
        project_kernel,
        out_shape=jax.ShapeDtypeStruct((1, F, 256), jnp.float32),
        in_specs=[VMEM, VMEM],
        out_specs=VMEM,
        compiler_params=pltpu.CompilerParams(vmem_limit_bytes=4 << 20),
        name="project",
    )(sums, kernel)


def prefetch_kernel(kernel_ref, out_ref, done):
    copy = pltpu.make_async_copy(kernel_ref, out_ref, done)
    copy.start()
    copy.wait()


def prefetch(kernel):
    return pl.pallas_call(
        prefetch_kernel,
        out_shape=jax.ShapeDtypeStruct(kernel.shape, kernel.dtype),
        in_specs=[pl.BlockSpec(memory_space=pl.ANY)],
        out_specs=VMEM,
        scratch_shapes=[pltpu.SemaphoreType.DMA],
        compiler_params=pltpu.CompilerParams(vmem_limit_bytes=4 << 20),
        cost_estimate=pl.CostEstimate(
            flops=0, bytes_accessed=2 * kernel.size * 2, transcendentals=0
        ),
        name="prefetch",
    )(kernel)


def on_device(spectra, pair_bins, row_subs, station_subs, kernel):
    z, core, y, x = [lax.axis_index(a) for a in AXES]
    row = z * NCORE + core

    packed = pack(spectra, pair_bins)
    packed = [packed[0]] + [shift(packed[d], "y", d) for d in range(1, NY)]

    subs = jnp.arange(PS, dtype=jnp.int32)
    sub_at = (subs % 32 // 4) * 16 + subs % 4 * 4 + subs // 32
    slot_subs = row_subs[0]
    row_members = lax.dynamic_slice_in_dim(station_subs.T, row * NI, NI, 1)
    rowmask = jnp.any(row_members[None] == sub_at[:, None, None], axis=1)
    rowmask = jnp.where(subs[:, None] < NSUB, rowmask.astype(jnp.float32), 0.0)
    members = lax.dynamic_index_in_dim(
        station_subs.reshape(8, NY, NX, ST, 8), x, 2, keepdims=False
    )
    members = members.transpose(3, 1, 0, 2).reshape(8, NJ)
    hit = jnp.any(members[None] == slot_subs[:, None, None], axis=0)
    place = members % 4 * 32 + members // 16 * 4 + members // 4 % 4
    kth = jnp.arange(8, dtype=jnp.int32)
    rank = jnp.sum(hit[None] & (kth[None, :, None] < kth[:, None, None]), axis=1)
    at_rank = hit[None] & (rank[None] == kth[:, None, None])
    slots = NSUB + jnp.sum(jnp.where(at_rank, place[None] - NSUB, 0), axis=1)
    slots = jnp.pad(slots, ((0, 0), (0, PJ - NJ)), constant_values=NSUB)
    counts = jnp.sum(hit.astype(jnp.int32), axis=0)
    columns = jnp.arange(NJ, dtype=jnp.int32)
    used, many = counts > 0, counts > 4
    key = jnp.where(used, jnp.where(many, columns, columns + NJ), columns + 2 * NJ)
    before = jnp.sum(key[:, None] < key[None, :], axis=0)
    places = jnp.arange(PL, dtype=jnp.int32)
    at_place = used[:, None] & (before[:, None] == places[None, :])
    entries = jnp.where(at_place, columns[:, None] - NJ, 0)
    entries = jnp.where(places[None, :] == PL - 1, used[:, None].astype(jnp.int32), entries)
    entries = jnp.where(places[None, :] == PL - 2, many[:, None].astype(jnp.int32), entries)
    listed = NJ + jnp.sum(entries, axis=0, keepdims=True)

    mine = jnp.stack([p[: FG * ST].reshape(FG, ST, T) for p in packed])
    mine, listed, slots, rowmask = lax.optimization_barrier((mine, listed, slots, rowmask))
    row_pieces = [mine] + [shift(mine, "x", d) for d in range(1, NX)]
    col_pieces = [mine] + [shift(mine, "z", d) for d in range(1, NZ)]
    col_pieces += [shift(p, "core", 1) for p in col_pieces]

    row_pieces[2], rowmask = lax.optimization_barrier((row_pieces[2], rowmask))
    kept, passed = binning(listed, slots, row_pieces, col_pieces, *tables(packed, rowmask))
    own, *sums = add_cores(kept, shift(passed, "core", 1))
    *sums, kernel = lax.optimization_barrier((*sums, kernel))
    kernel = prefetch(kernel)
    received = [shift(sums[d - 1], "x", d) for d in range(1, NX)]
    kernel, *received = lax.optimization_barrier((kernel, *received))
    for part in received:
        own = own + part.astype(jnp.float32)
    both = lax.all_to_all(own.astype(jnp.bfloat16), ("z", "y"), 0, 0, tiled=True)
    return project(both, kernel)


def solution(mesh):
    chips = jax.sharding.Mesh(mesh.devices.reshape(NZ, NCORE, NY, NX), AXES)
    in_specs = (P(AXES, None, None), P(AXES[:2], AXES[2:]), P(AXES[:2], None), P(), P())
    out_specs = P(AXES, None, None)
    return jax.shard_map(
        on_device, mesh=chips, in_specs=in_specs, out_specs=out_specs, check_vma=False
    )
```
